32 devices in a mesh: replica: 4 (over y, x), shard: 8 (over z, core).
Axes of the slice: x: 2, y: 2, z: 4, core: 2. Of those that a mesh axis runs over, the one named last changes fastest.
Arguments:
- tokens: bfloat16 [4096, 8192], P(('replica', 'shard')), may hold values from -6 to 6
- cotangent: bfloat16 [4096, 512], P(('replica', 'shard')), may hold values from -6 to 6
- biased: float32 [4, 8192, 512], P('replica', 'shard'), may hold values from -0.0625 to 0.0625
- momentum: float32 [4, 8192, 512], P('replica', 'shard'), may hold values from -0.12 to 0.12
- weight: float32 [4], P('replica'), may hold values from 0.25 to 4
- round_index: int32 [1], replicated, may hold values from 0 to 999999
Outputs:
- projected: bfloat16 [4096, 512], P(('replica', 'shard'))
- mixed: float32 [4, 8192, 512], P('replica', 'shard')
- weight_out: float32 [4], P('replica')
- velocity: float32 [4, 8192, 512], P('replica', 'shard')
- debiased: float32 [4, 8192, 512], P('replica', 'shard')
The draws below stay inside these ranges and needn't reach their ends.
Inputs may be any that keep to these rules, and one draw needn't show every extreme that they name: `round_index`: any round number.
All inputs are finite; a program needn't handle non-finite values.
Results may differ from the reference program's by a relative error of at most 0.005.
Values may be sent and summed in bfloat16 or wider, within the bound.
A program may use at most 64 MiB of HBM per device.

```python
import math
import jax
import jax.numpy as jnp
from jax import lax

D = 8192
KV = 512
REP_TOK = 1024
TOKENS = 4096
HOPS = 2
N_REPLICA = 4


def steps_of(stream_key, shape, shards, low, top_value):
    def one(position, parts):
        heights = jax.random.uniform(jax.random.fold_in(jax.random.fold_in(stream_key, 6), position), (parts,), jnp.float32, low / len(shards), top_value / len(shards))
        return jnp.repeat(jnp.exp(heights), shape[position] // parts).reshape((-1,) + (1,) * (len(shape) - position - 1))

    gain = one(*shards[0])
    for cut in shards[1:]:
        gain = gain * one(*cut)
    return gain


def gaussian(key, dims, deviation, reach, split=(), kind=jnp.bfloat16):
    level = steps_of(key, dims, split, -0.22, 0.18) if split else 1.0
    drawn = jax.random.normal(key, dims, jnp.float32) * deviation * level
    return jnp.minimum(jnp.maximum(drawn, -reach), reach).astype(kind)


def setup_inputs(seed: int = 0) -> dict:
    streams_of = jax.random.split(jax.random.key(seed), 7)
    return {
        "tokens": gaussian(streams_of[0], (TOKENS, D), 1.0, 6.0, ((0, 32),)),
        "cotangent": gaussian(streams_of[1], (TOKENS, KV), 1.0, 6.0, ((0, 32),)),
        "biased": gaussian(streams_of[2], (N_REPLICA, D, KV), D ** -0.5, 0.0625, ((0, 4), (1, 8)), jnp.float32),
        "momentum": gaussian(streams_of[3], (N_REPLICA, D, KV), 0.02, 0.12, ((0, 4), (1, 8)), jnp.float32),
        "weight": jnp.clip(jnp.exp(math.log(4.0) - 2.7725887 * jax.random.uniform(streams_of[4], (N_REPLICA,), jnp.float32) ** steps_of(streams_of[4], (N_REPLICA,), ((0, 4),), -0.2, 0.2)), 0.25, 4.0),
        "round_index": jax.random.randint(streams_of[5], (1,), 0, 1000000).astype(jnp.int32),
    }


MOMENT = 0.9
LEARN = 0.5


def reference(tokens, cotangent, biased, momentum, weight, round_index):
    tok_rep = tokens.reshape(N_REPLICA, REP_TOK, D)
    cot_rep = cotangent.reshape(N_REPLICA, REP_TOK, KV)

    def replica_work(items):
        rows, cots, numer, veloc, scale = items
        current = (numer / scale).astype(jnp.bfloat16)
        output = jnp.dot(rows, current, preferred_element_type=jnp.float32).astype(jnp.bfloat16)
        gradient = lax.dot_general(rows, cots, (((0,), (0,)), ((), ())), preferred_element_type=jnp.float32) / REP_TOK
        new_veloc = MOMENT * veloc + gradient
        stepped = numer - LEARN * (gradient + MOMENT * new_veloc)
        return output, stepped, new_veloc

    output, stepped, velocity = lax.map(replica_work, (tok_rep, cot_rep, biased, momentum, weight))
    power = (round_index[0] % HOPS).astype(jnp.int32)
    dist = jnp.left_shift(jnp.int32(1), power)
    source = (jnp.arange(N_REPLICA, dtype=jnp.int32) - dist) % N_REPLICA
    mixed = 0.5 * (stepped + stepped[source])
    weight_out = 0.5 * (weight + weight[source])
    debiased = mixed / weight_out[:, None, None]
    return output.reshape(TOKENS, KV), mixed, weight_out, velocity, debiased
```

```python
from functools import partial

import jax
import jax.numpy as jnp
from jax import lax
from jax.experimental import pallas as pl
from jax.experimental.pallas import tpu as pltpu
from jax.sharding import PartitionSpec as P

MOMENT = 0.9
LEARN = 0.5
MESH = pl.DeviceIdType.MESH
CORES = 2
BF16 = jnp.bfloat16
F32 = jnp.float32


def flipped(z, x, chips):
    total, bit = 0, 1
    while bit < chips:
        total = total + bit * ((z // bit + x // bit) % 2)
        bit *= 2
    return total


def partners(chips):
    order, bit = [], chips // 2
    while bit >= 1:
        order += list(range(bit, 2 * bit))
        bit //= 2
    return order


def push_kernel(dist, chips, nk, tok, cot, biased, momentum, weight,
                p_out, g_out, s_out, w_out,
                t_v, c_v, b_v, m_v, cur, acc, p_send, p_recv, gp_send, gp_recv, g_v, s_send, w_send,
                load_sem, own_sem, c_ssem, c_rsem, t_ssem, t_rsem, cur_ssem, cur_rsem,
                gp_ssem, gp_rsem, s_ssem, s_rsem, p_ssem, p_rsem, w_ssem, w_rsem, store_sem):
    rows, kv = b_v.shape
    own_tok = tok.shape[0]
    width = rows // nk
    rep_tok = own_tok * chips * CORES
    replicas = lax.axis_size("replica")
    rep = lax.axis_index("replica")
    shard = lax.axis_index("shard")
    z = shard // CORES
    c = shard % CORES
    other = 1 - c
    mate = z * CORES + other
    ahead = (rep + dist) % replicas
    behind = (rep + replicas - dist) % replicas
    order = partners(chips)
    peers = [flipped(z, x, chips) for x in order]

    loads = [
        pltpu.make_async_copy(biased, b_v, load_sem.at[0]),
        pltpu.make_async_copy(momentum, m_v, load_sem.at[1]),
        pltpu.make_async_copy(cot, c_v.at[z], load_sem.at[2]),
    ]
    for load in loads:
        load.start()

    def columns(chip, half, k):
        return pl.ds(pl.multiple_of((chip * CORES + half) * rows + k * width, width), width)

    def own_copy(k, half):
        return pltpu.make_async_copy(tok.at[:, columns(z, half, k)], t_v.at[k, half, z], own_sem.at[k, half])

    def tok_copy(k, half, j):
        return pltpu.make_async_remote_copy(
            src_ref=tok.at[:, columns(peers[j], half, k)], dst_ref=t_v.at[k, half, z],
            send_sem=t_ssem.at[k, half, j], recv_sem=t_rsem.at[k, half, j],
            device_id={"shard": peers[j] * CORES + c}, device_id_type=MESH)

    def cot_copy(j):
        return pltpu.make_async_remote_copy(
            src_ref=cot, dst_ref=c_v.at[z], send_sem=c_ssem.at[j], recv_sem=c_rsem.at[j],
            device_id={"shard": peers[j] * CORES + c}, device_id_type=MESH)

    def p_copy(j):
        return pltpu.make_async_remote_copy(
            src_ref=p_send.at[j], dst_ref=p_recv.at[j], send_sem=p_ssem.at[j], recv_sem=p_rsem.at[j],
            device_id={"shard": peers[j] * CORES + c}, device_id_type=MESH)

    def gp_copy(k):
        return pltpu.make_async_remote_copy(
            src_ref=gp_send.at[k], dst_ref=gp_recv.at[k], send_sem=gp_ssem.at[k], recv_sem=gp_rsem.at[k],
            device_id={"shard": mate}, device_id_type=MESH)

    def s_copy(k):
        return pltpu.make_async_remote_copy(
            src_ref=s_send.at[k], dst_ref=s_out.at[pl.ds(pl.multiple_of(k * width, width), width), :],
            send_sem=s_ssem.at[k], recv_sem=s_rsem.at[k],
            device_id={"replica": ahead}, device_id_type=MESH)

    def g_store(k):
        return pltpu.make_async_copy(
            g_v.at[k], g_out.at[pl.ds(pl.multiple_of(k * width, width), width), :], store_sem.at[k])

    for k in range(nk):
        for half in range(CORES):
            own_copy(k, half).start()

    barrier = pltpu.get_barrier_semaphore()
    for peer in peers:
        pl.semaphore_signal(barrier, inc=1, device_id={"shard": peer * CORES + c}, device_id_type=MESH)
    pl.semaphore_signal(barrier, inc=1, device_id={"shard": mate}, device_id_type=MESH)
    pl.semaphore_signal(barrier, inc=1, device_id={"replica": behind}, device_id_type=MESH)
    pl.semaphore_wait(barrier, len(peers) + 2)

    for j in range(len(peers)):
        cot_copy(j).start()
    for k in range(nk):
        for j in range(len(peers)):
            for half in range(CORES):
                tok_copy(k, half, j).start()

    w_send[...] = jnp.full(w_send.shape, weight[0], F32)
    w_copy = pltpu.make_async_remote_copy(
        src_ref=w_send, dst_ref=w_out, send_sem=w_ssem, recv_sem=w_rsem,
        device_id={"replica": ahead}, device_id_type=MESH)
    w_copy.start()

    loads[0].wait()
    mine = cur.at[c]
    mine[...] = (b_v[...] / weight[0]).astype(BF16)
    cur_copy = pltpu.make_async_remote_copy(
        src_ref=mine, dst_ref=mine, send_sem=cur_ssem, recv_sem=cur_rsem,
        device_id={"shard": mate}, device_id_type=MESH)
    cur_copy.start()
    acc[...] = jnp.zeros(acc.shape, F32)
    loads[1].wait()
    loads[2].wait()
    for j in range(len(peers)):
        cot_copy(j).wait_recv()
    cur_copy.wait_recv()

    contract = (((0,), (0,)), ((), ()))

    def arrived(k):
        for half in range(CORES):
            own_copy(k, half).wait()
        for j in range(len(peers)):
            for half in range(CORES):
                tok_copy(k, half, j).wait_recv()

    def partial_gradient(k, half):
        t = t_v[k, half].reshape(chips * own_tok, width)
        cots = c_v[...].reshape(chips * own_tok, kv)
        return lax.dot_general(t, cots, contract, preferred_element_type=F32)

    def product(k, t):
        here = pl.ds(pl.multiple_of(k * width, width), width)
        return (jnp.dot(t[0], cur[0, here, :], preferred_element_type=F32)
                + jnp.dot(t[1], cur[1, here, :], preferred_element_type=F32))

    def send_gradient(k):
        gp_send[k] = partial_gradient(k, other).astype(BF16)
        gp_copy(k).start()
        g_v[k] = partial_gradient(k, c)

    def finish_gradient(k):
        here = pl.ds(pl.multiple_of(k * width, width), width)
        gp_copy(k).wait_recv()
        gradient = (g_v[k] + gp_recv[k].astype(F32)) / rep_tok
        g_v[k] = gradient
        velocity = MOMENT * m_v[here, :] + gradient
        s_send[k] = (b_v[here, :] - LEARN * (gradient + MOMENT * velocity)).astype(BF16)
        s_copy(k).start()
        g_store(k).start()

    if nk > 1:
        @pl.loop(0, nk - 1)
        def _(k):
            arrived(k)
            send_gradient(k)
            for s in range(chips):
                acc[s] += product(k, (t_v[k, 0, s], t_v[k, 1, s]))
            finish_gradient(k)

    last = nk - 1
    arrived(last)
    send_gradient(last)
    for j in range(len(peers)):
        s = peers[j]
        p_send[j] = (acc[s] + product(last, (t_v[last, 0, s], t_v[last, 1, s]))).astype(BF16)
        p_copy(j).start()
    finish_gradient(last)
    total = acc[z] + product(last, (t_v[last, 0, z], t_v[last, 1, z]))
    for j in range(len(peers)):
        p_copy(j).wait_recv()
        total = total + p_recv[j].astype(F32)
    p_send[len(peers)] = total.astype(BF16)
    p_store = pltpu.make_async_copy(p_send.at[len(peers)], p_out, store_sem.at[nk])
    p_store.start()

    for j in range(len(peers)):
        cot_copy(j).wait_send()
        p_copy(j).wait_send()
        for k in range(nk):
            for half in range(CORES):
                tok_copy(k, half, j).wait_send()
    cur_copy.wait_send()
    for k in range(nk):
        gp_copy(k).wait_send()
        s_copy(k).wait()
        g_store(k).wait()
    w_copy.wait()
    p_store.wait()


def push_call(level, chips, tokens, cotangent, numer, moment, weight):
    own_tok, features = tokens.shape
    rows, kv = numer.shape
    nk = max(1, rows // 256)
    width = rows // nk
    n = chips - 1
    any_spec = pl.BlockSpec(memory_space=pl.ANY)
    dma = pltpu.SemaphoreType.DMA
    return pl.pallas_call(
        partial(push_kernel, 1 << level, chips, nk),
        out_shape=(
            jax.ShapeDtypeStruct((own_tok, kv), BF16),
            jax.ShapeDtypeStruct((rows, kv), F32),
            jax.ShapeDtypeStruct((rows, kv), BF16),
            jax.ShapeDtypeStruct((8, 128), F32),
        ),
        in_specs=[any_spec] * 4 + [pl.BlockSpec(memory_space=pltpu.SMEM)],
        out_specs=[any_spec] * 4,
        scratch_shapes=[
            pltpu.VMEM((nk, CORES, chips, own_tok, width), BF16),
            pltpu.VMEM((chips, own_tok, kv), BF16),
            pltpu.VMEM((rows, kv), F32),
            pltpu.VMEM((rows, kv), F32),
            pltpu.VMEM((CORES, rows, kv), BF16),
            pltpu.VMEM((chips, own_tok, kv), F32),
            pltpu.VMEM((chips, own_tok, kv), BF16),
            pltpu.VMEM((n, own_tok, kv), BF16),
            pltpu.VMEM((nk, width, kv), BF16),
            pltpu.VMEM((nk, width, kv), BF16),
            pltpu.VMEM((nk, width, kv), F32),
            pltpu.VMEM((nk, width, kv), BF16),
            pltpu.VMEM((8, 128), F32),
            dma((3,)), dma((nk, CORES)), dma((n,)), dma((n,)), dma((nk, CORES, n)), dma((nk, CORES, n)),
            dma(()), dma(()), dma((nk,)), dma((nk,)), dma((nk,)), dma((nk,)), dma((n,)), dma((n,)),
            dma(()), dma(()), dma((nk + 1,)),
        ],
        compiler_params=pltpu.CompilerParams(
            collective_id=level, has_side_effects=True, vmem_limit_bytes=48 * 1024 * 1024),
        cost_estimate=pl.CostEstimate(
            flops=4 * own_tok * features * kv, bytes_accessed=12 * rows * kv, transcendentals=0),
        name=f"push_round_{level}",
    )(tokens, cotangent, numer, moment, weight)


def shards(tokens, cotangent, biased, momentum, weight, round_index):
    hops = lax.axis_size("replica").bit_length() - 1
    chips = lax.axis_size("shard") // CORES
    power = round_index[0] % hops
    numer = biased[0]
    moment = momentum[0]
    branches = [partial(push_call, level, chips) for level in range(hops)]
    output, gradient, stepped_from, weight_from = lax.switch(
        power, branches, tokens, cotangent, numer, moment, weight)
    velocity = MOMENT * moment + gradient
    stepped = numer - LEARN * (gradient + MOMENT * velocity)
    mixed = 0.5 * (stepped + stepped_from.astype(F32))
    weight_out = 0.5 * (weight + weight_from[0, :1])
    debiased = mixed / weight_out[0]
    return (output, mixed[None], weight_out, velocity[None], debiased[None])


def solution(mesh):
    placed = (
        P(("replica", "shard"), None),
        P(("replica", "shard"), None),
        P("replica", "shard", None),
        P("replica", "shard", None),
        P("replica"),
        P(),
    )
    return jax.shard_map(
        shards,
        mesh=mesh,
        in_specs=placed,
        out_specs=(
            P(("replica", "shard"), None),
            P("replica", "shard", None),
            P("replica"),
            P("replica", "shard", None),
            P("replica", "shard", None),
        ),
        check_vma=False,
    )
```

```python
from functools import partial

import jax
import jax.numpy as jnp
from jax import lax
from jax.experimental import pallas as pl
from jax.experimental.pallas import tpu as pltpu
from jax.sharding import PartitionSpec as P

MOMENT = 0.9
LEARN = 0.5
MESH = pl.DeviceIdType.MESH
CORES = 2
BF16 = jnp.bfloat16
F32 = jnp.float32


def flipped(z, x, chips):
    total, bit = 0, 1
    while bit < chips:
        total = total + bit * ((z // bit + x // bit) % 2)
        bit *= 2
    return total


def partners(chips):
    order, bit = [], chips // 2
    while bit >= 1:
        order += list(range(bit, 2 * bit))
        bit //= 2
    return order


def push_kernel(dist, chips, nk, tok, cot, biased, momentum, weight,
                p_out, mix_out, w_out, vel_out, deb_out,
                t_v, c_v, b_v, m_v, cur, acc, p_send, p_recv, gp_send, gp_recv, g_v, s_send, s_recv, deb_v,
                w_send, w_recv,
                load_sem, own_sem, c_ssem, c_rsem, t_ssem, t_rsem, cur_ssem, cur_rsem,
                gp_ssem, gp_rsem, s_ssem, s_rsem, p_ssem, p_rsem, w_ssem, w_rsem, store_sem):
    rows, kv = b_v.shape
    own_tok = tok.shape[0]
    width = rows // nk
    rep_tok = own_tok * chips * CORES
    replicas = lax.axis_size("replica")
    rep = lax.axis_index("replica")
    shard = lax.axis_index("shard")
    z = shard // CORES
    c = shard % CORES
    other = 1 - c
    mate = z * CORES + other
    ahead = (rep + dist) % replicas
    behind = (rep + replicas - dist) % replicas
    order = partners(chips)
    peers = [flipped(z, x, chips) for x in order]

    loads = [
        pltpu.make_async_copy(biased, b_v, load_sem.at[0]),
        pltpu.make_async_copy(momentum, m_v, load_sem.at[1]),
        pltpu.make_async_copy(cot, c_v.at[z], load_sem.at[2]),
    ]
    for load in loads:
        load.start()

    def columns(chip, half, k):
        return pl.ds(pl.multiple_of((chip * CORES + half) * rows + k * width, width), width)

    def own_copy(k, half):
        return pltpu.make_async_copy(tok.at[:, columns(z, half, k)], t_v.at[k, half, z], own_sem.at[k, half])

    def tok_copy(k, half, j):
        return pltpu.make_async_remote_copy(
            src_ref=tok.at[:, columns(peers[j], half, k)], dst_ref=t_v.at[k, half, z],
            send_sem=t_ssem.at[k, half, j], recv_sem=t_rsem.at[k, half, j],
            device_id={"shard": peers[j] * CORES + c}, device_id_type=MESH)

    def cot_copy(x):
        low = x & -x
        held = z if x == low else flipped(z, x - low, chips)
        return pltpu.make_async_remote_copy(
            src_ref=c_v.at[held], dst_ref=c_v.at[held], send_sem=c_ssem.at[x], recv_sem=c_rsem.at[x],
            device_id={"shard": flipped(z, low, chips) * CORES + c}, device_id_type=MESH)

    def p_copy(j):
        return pltpu.make_async_remote_copy(
            src_ref=p_send.at[j], dst_ref=p_recv.at[j], send_sem=p_ssem.at[j], recv_sem=p_rsem.at[j],
            device_id={"shard": peers[j] * CORES + c}, device_id_type=MESH)

    def gp_copy(k):
        return pltpu.make_async_remote_copy(
            src_ref=gp_send.at[k], dst_ref=gp_recv.at[k], send_sem=gp_ssem.at[k], recv_sem=gp_rsem.at[k],
            device_id={"shard": mate}, device_id_type=MESH)

    def s_copy(k):
        return pltpu.make_async_remote_copy(
            src_ref=s_send.at[k], dst_ref=s_recv.at[k],
            send_sem=s_ssem.at[k], recv_sem=s_rsem.at[k],
            device_id={"replica": ahead}, device_id_type=MESH)

    def store(k, i):
        here = pl.ds(pl.multiple_of(k * width, width), width)
        made, out = ((m_v, vel_out), (b_v, mix_out), (deb_v, deb_out))[i]
        return pltpu.make_async_copy(made.at[here, :], out.at[here, :], store_sem.at[k, i])

    for k in range(nk):
        for half in range(CORES):
            own_copy(k, half).start()

    barrier = pltpu.get_barrier_semaphore()
    for peer in peers:
        pl.semaphore_signal(barrier, inc=1, device_id={"shard": peer * CORES + c}, device_id_type=MESH)
    pl.semaphore_signal(barrier, inc=1, device_id={"shard": mate}, device_id_type=MESH)
    pl.semaphore_signal(barrier, inc=1, device_id={"replica": behind}, device_id_type=MESH)
    pl.semaphore_wait(barrier, len(peers) + 2)

    loads[2].wait()
    cot_copy(chips // 2).start()
    for k in range(nk):
        for j in range(len(peers)):
            for half in range(CORES):
                tok_copy(k, half, j).start()

    w_send[...] = jnp.full(w_send.shape, weight[0], F32)
    w_copy = pltpu.make_async_remote_copy(
        src_ref=w_send, dst_ref=w_recv, send_sem=w_ssem, recv_sem=w_rsem,
        device_id={"replica": ahead}, device_id_type=MESH)
    w_copy.start()

    loads[0].wait()
    mine = cur.at[c]
    mine[...] = (b_v[...] / weight[0]).astype(BF16)
    cur_copy = pltpu.make_async_remote_copy(
        src_ref=mine, dst_ref=mine, send_sem=cur_ssem, recv_sem=cur_rsem,
        device_id={"shard": mate}, device_id_type=MESH)
    cur_copy.start()
    acc[...] = jnp.zeros(acc.shape, F32)
    loads[1].wait()
    bit = chips // 4
    while bit >= 1:
        for x in range(2 * bit, chips, 4 * bit):
            cot_copy(x).wait_recv()
        for x in range(bit, chips, 2 * bit):
            cot_copy(x).start()
        bit //= 2
    for x in range(1, chips, 2):
        cot_copy(x).wait_recv()
    cur_copy.wait_recv()
    w_copy.wait()
    w_send[...] = 0.5 * (w_send[...] + w_recv[...])
    w_store = pltpu.make_async_copy(w_send, w_out, w_ssem)
    w_store.start()

    contract = (((0,), (0,)), ((), ()))

    def arrived(k):
        for half in range(CORES):
            own_copy(k, half).wait()
        for j in range(len(peers)):
            for half in range(CORES):
                tok_copy(k, half, j).wait_recv()

    def partial_gradient(k, half):
        t = t_v[k, half].reshape(chips * own_tok, width)
        cots = c_v[...].reshape(chips * own_tok, kv)
        return lax.dot_general(t, cots, contract, preferred_element_type=F32)

    def product(k, t):
        here = pl.ds(pl.multiple_of(k * width, width), width)
        return (jnp.dot(t[0], cur[0, here, :], preferred_element_type=F32)
                + jnp.dot(t[1], cur[1, here, :], preferred_element_type=F32))

    def send_gradient(k):
        gp_send[k] = partial_gradient(k, other).astype(BF16)
        gp_copy(k).start()
        g_v[k] = partial_gradient(k, c)

    def finish_gradient(k):
        here = pl.ds(pl.multiple_of(k * width, width), width)
        gp_copy(k).wait_recv()
        gradient = (g_v[k] + gp_recv[k].astype(F32)) / rep_tok
        velocity = MOMENT * m_v[here, :] + gradient
        m_v[here, :] = velocity
        stepped = b_v[here, :] - LEARN * (gradient + MOMENT * velocity)
        b_v[here, :] = stepped
        s_send[k] = stepped.astype(BF16)
        s_copy(k).start()
        store(k, 0).start()

    def mix(k):
        here = pl.ds(pl.multiple_of(k * width, width), width)
        s_copy(k).wait_recv()
        mixed = 0.5 * (b_v[here, :] + s_recv[k].astype(F32))
        b_v[here, :] = mixed
        deb_v[here, :] = mixed / w_send[0:1, 0:1]
        store(k, 1).start()
        store(k, 2).start()

    if nk > 1:
        @pl.loop(0, nk - 1)
        def _(k):
            arrived(k)
            send_gradient(k)
            for s in range(chips):
                acc[s] += product(k, (t_v[k, 0, s], t_v[k, 1, s]))
            finish_gradient(k)

            @pl.when(k >= 2)
            def _():
                mix(k - 2)

    last = nk - 1
    arrived(last)
    send_gradient(last)
    for j in range(len(peers)):
        s = peers[j]
        p_send[j] = (acc[s] + product(last, (t_v[last, 0, s], t_v[last, 1, s]))).astype(BF16)
        p_copy(j).start()
    finish_gradient(last)
    for k in range(max(0, nk - 3), last):
        mix(k)
    total = acc[z] + product(last, (t_v[last, 0, z], t_v[last, 1, z]))
    for j in range(len(peers)):
        p_copy(j).wait_recv()
        total = total + p_recv[j].astype(F32)
    p_send[len(peers)] = total.astype(BF16)
    p_store = pltpu.make_async_copy(p_send.at[len(peers)], p_out, store_sem.at[nk, 0])
    p_store.start()
    mix(last)

    for j in range(len(peers)):
        cot_copy(j + 1).wait_send()
        p_copy(j).wait_send()
        for k in range(nk):
            for half in range(CORES):
                tok_copy(k, half, j).wait_send()
    cur_copy.wait_send()
    for k in range(nk):
        gp_copy(k).wait_send()
        s_copy(k).wait_send()
        for i in range(3):
            store(k, i).wait()
    w_store.wait()
    p_store.wait()


def push_call(level, chips, tokens, cotangent, numer, moment, weight):
    own_tok, features = tokens.shape
    rows, kv = numer.shape
    nk = max(1, rows // 256)
    width = rows // nk
    n = chips - 1
    any_spec = pl.BlockSpec(memory_space=pl.ANY)
    dma = pltpu.SemaphoreType.DMA
    return pl.pallas_call(
        partial(push_kernel, 1 << level, chips, nk),
        out_shape=(
            jax.ShapeDtypeStruct((own_tok, kv), BF16),
            jax.ShapeDtypeStruct((rows, kv), F32),
            jax.ShapeDtypeStruct((8, 128), F32),
            jax.ShapeDtypeStruct((rows, kv), F32),
            jax.ShapeDtypeStruct((rows, kv), F32),
        ),
        in_specs=[any_spec] * 4 + [pl.BlockSpec(memory_space=pltpu.SMEM)],
        out_specs=[any_spec] * 5,
        scratch_shapes=[
            pltpu.VMEM((nk, CORES, chips, own_tok, width), BF16),
            pltpu.VMEM((chips, own_tok, kv), BF16),
            pltpu.VMEM((rows, kv), F32),
            pltpu.VMEM((rows, kv), F32),
            pltpu.VMEM((CORES, rows, kv), BF16),
            pltpu.VMEM((chips, own_tok, kv), F32),
            pltpu.VMEM((chips, own_tok, kv), BF16),
            pltpu.VMEM((n, own_tok, kv), BF16),
            pltpu.VMEM((nk, width, kv), BF16),
            pltpu.VMEM((nk, width, kv), BF16),
            pltpu.VMEM((nk, width, kv), F32),
            pltpu.VMEM((nk, width, kv), BF16),
            pltpu.VMEM((nk, width, kv), BF16),
            pltpu.VMEM((rows, kv), F32),
            pltpu.VMEM((8, 128), F32),
            pltpu.VMEM((8, 128), F32),
            dma((3,)), dma((nk, CORES)), dma((chips,)), dma((chips,)), dma((nk, CORES, n)), dma((nk, CORES, n)),
            dma(()), dma(()), dma((nk,)), dma((nk,)), dma((nk,)), dma((nk,)), dma((n,)), dma((n,)),
            dma(()), dma(()), dma((nk + 1, 3)),
        ],
        compiler_params=pltpu.CompilerParams(
            collective_id=level, has_side_effects=True, vmem_limit_bytes=48 * 1024 * 1024),
        cost_estimate=pl.CostEstimate(
            flops=4 * own_tok * features * kv, bytes_accessed=12 * rows * kv, transcendentals=0),
        name=f"push_round_{level}",
    )(tokens, cotangent, numer, moment, weight)


def hand_out_kernel(p, mix, w, vel, deb, p_out, mix_out, w_out, vel_out, deb_out, w_v, sem):
    copies = [
        pltpu.make_async_copy(made, out, sem.at[i])
        for i, (made, out) in enumerate(((w, w_v), (mix, mix_out), (vel, vel_out), (deb, deb_out), (p, p_out)))
    ]
    for copy in copies:
        copy.start()
    copies[0].wait()
    w_out[0] = jnp.max(w_v[...])
    for copy in copies[1:]:
        copy.wait()


def hand_out(p, mix, w, vel, deb):
    any_spec = pl.BlockSpec(memory_space=pl.ANY)
    hbm = pl.BlockSpec(memory_space=pltpu.HBM)
    like = lambda a: jax.ShapeDtypeStruct(a.shape, a.dtype)
    return pl.pallas_call(
        hand_out_kernel,
        out_shape=(like(p), like(mix), jax.ShapeDtypeStruct((1,), F32), like(vel), like(deb)),
        in_specs=[any_spec] * 5,
        out_specs=[hbm, hbm, pl.BlockSpec(memory_space=pltpu.SMEM), hbm, hbm],
        scratch_shapes=[pltpu.VMEM((8, 128), F32), pltpu.SemaphoreType.DMA((5,))],
        cost_estimate=pl.CostEstimate(flops=0, bytes_accessed=12 * mix.size, transcendentals=0),
        name="hand_out",
    )(p, mix, w, vel, deb)


def shards(tokens, cotangent, biased, momentum, weight, round_index):
    hops = lax.axis_size("replica").bit_length() - 1
    chips = lax.axis_size("shard") // CORES
    power = round_index[0] % hops
    branches = [partial(push_call, level, chips) for level in range(hops)]
    made = lax.switch(power, branches, tokens, cotangent, biased[0], momentum[0], weight)
    output, mixed, weight_out, velocity, debiased = hand_out(*made)
    return (output, mixed[None], weight_out, velocity[None], debiased[None])


def solution(mesh):
    placed = (
        P(("replica", "shard"), None),
        P(("replica", "shard"), None),
        P("replica", "shard", None),
        P("replica", "shard", None),
        P("replica"),
        P(),
    )
    return jax.shard_map(
        shards,
        mesh=mesh,
        in_specs=placed,
        out_specs=(
            P(("replica", "shard"), None),
            P("replica", "shard", None),
            P("replica"),
            P("replica", "shard", None),
            P("replica", "shard", None),
        ),
        check_vma=False,
    )
```

```python
from functools import partial

import jax
import jax.numpy as jnp
from jax import lax
from jax.experimental import pallas as pl
from jax.experimental.pallas import tpu as pltpu
from jax.sharding import PartitionSpec as P

MOMENT = 0.9
LEARN = 0.5
MESH = pl.DeviceIdType.MESH
CORES = 2
BF16 = jnp.bfloat16
F32 = jnp.float32


def flipped(z, x, chips):
    total, bit = 0, 1
    while bit < chips:
        total = total + bit * ((z // bit + x // bit) % 2)
        bit *= 2
    return total


def partners(chips):
    order, bit = [], chips // 2
    while bit >= 1:
        order += list(range(bit, 2 * bit))
        bit //= 2
    return order


def push_kernel(dist, chips, nk, look, tok, cot, biased, momentum, weight,
                p_out, mix_out, w_out, vel_out, deb_out,
                t_v, c_v, b_v, m_v, cur, acc, p_send, p_recv, gp_send, gp_recv, g_v, s_send, s_recv, deb_v,
                w_send, w_recv,
                load_sem, own_sem, c_ssem, c_rsem, t_ssem, t_rsem, e_ssem, e_rsem, cur_ssem, cur_rsem,
                gp_ssem, gp_rsem, s_ssem, s_rsem, p_ssem, p_rsem, w_ssem, w_rsem, store_sem):
    rows, kv = b_v.shape
    own_tok = tok.shape[0]
    width = rows // nk
    last = nk - 1
    nt, block = p_send.shape[1], p_send.shape[2]
    early = min(2, last)
    rep_tok = own_tok * chips * CORES
    replicas = lax.axis_size("replica")
    rep = lax.axis_index("replica")
    shard = lax.axis_index("shard")
    z = shard // CORES
    c = shard % CORES
    other = 1 - c
    mate = z * CORES + other
    ahead = (rep + dist) % replicas
    behind = (rep + replicas - dist) % replicas
    order = partners(chips)
    peers = [flipped(z, x, chips) for x in order]

    loads = [
        pltpu.make_async_copy(biased, b_v, load_sem.at[0]),
        pltpu.make_async_copy(momentum, m_v, load_sem.at[1]),
        pltpu.make_async_copy(cot, c_v.at[z], load_sem.at[2]),
    ]
    for load in loads:
        load.start()

    def columns(chip, half, k):
        return pl.ds(pl.multiple_of((chip * CORES + half) * rows + k * width, width), width)

    def own_copy(k, half):
        return pltpu.make_async_copy(tok.at[:, columns(z, half, k)], t_v.at[k, half, z], own_sem.at[k, half])

    def tok_copy(k, half, j):
        return pltpu.make_async_remote_copy(
            src_ref=tok.at[:, columns(peers[j], half, k)], dst_ref=t_v.at[k, half, z],
            send_sem=t_ssem.at[k, half, j], recv_sem=t_rsem.at[k, half, j],
            device_id={"shard": peers[j] * CORES + c}, device_id_type=MESH)

    def end_copy(t, half, j):
        part = pl.ds(t * block, block)
        return pltpu.make_async_remote_copy(
            src_ref=tok.at[part, columns(peers[j], half, last)], dst_ref=t_v.at[last, half, z, part],
            send_sem=e_ssem.at[t, half, j], recv_sem=e_rsem.at[t, half, j],
            device_id={"shard": peers[j] * CORES + c}, device_id_type=MESH)

    def send_chunk(k):
        for j in range(len(peers)):
            for half in range(CORES):
                tok_copy(k, half, j).start()

    def send_last():
        for t in range(nt):
            for j in range(len(peers)):
                for half in range(CORES):
                    end_copy(t, half, j).start()

    def cot_copy(x):
        low = x & -x
        held = z if x == low else flipped(z, x - low, chips)
        return pltpu.make_async_remote_copy(
            src_ref=c_v.at[held], dst_ref=c_v.at[held], send_sem=c_ssem.at[x], recv_sem=c_rsem.at[x],
            device_id={"shard": flipped(z, low, chips) * CORES + c}, device_id_type=MESH)

    def p_copy(x, t):
        return pltpu.make_async_remote_copy(
            src_ref=p_send.at[x, t], dst_ref=p_recv.at[x, t], send_sem=p_ssem.at[x, t], recv_sem=p_rsem.at[x, t],
            device_id={"shard": flipped(z, x & -x, chips) * CORES + c}, device_id_type=MESH)

    def gp_copy(k):
        return pltpu.make_async_remote_copy(
            src_ref=gp_send.at[k], dst_ref=gp_recv.at[k], send_sem=gp_ssem.at[k], recv_sem=gp_rsem.at[k],
            device_id={"shard": mate}, device_id_type=MESH)

    def s_copy(k):
        return pltpu.make_async_remote_copy(
            src_ref=s_send.at[k], dst_ref=s_recv.at[k],
            send_sem=s_ssem.at[k], recv_sem=s_rsem.at[k],
            device_id={"replica": ahead}, device_id_type=MESH)

    def store(k, i):
        here = pl.ds(pl.multiple_of(k * width, width), width)
        made, out = ((m_v, vel_out), (b_v, mix_out), (deb_v, deb_out))[i]
        return pltpu.make_async_copy(made.at[here, :], out.at[here, :], store_sem.at[k, i])

    for k in range(nk):
        for half in range(CORES):
            own_copy(k, half).start()

    barrier = pltpu.get_barrier_semaphore()
    for peer in peers:
        pl.semaphore_signal(barrier, inc=1, device_id={"shard": peer * CORES + c}, device_id_type=MESH)
    pl.semaphore_signal(barrier, inc=1, device_id={"shard": mate}, device_id_type=MESH)
    pl.semaphore_signal(barrier, inc=1, device_id={"replica": behind}, device_id_type=MESH)
    pl.semaphore_wait(barrier, len(peers) + 2)

    loads[2].wait()
    cot_copy(chips // 2).start()
    for k in range(early):
        send_chunk(k)

    w_send[...] = jnp.full(w_send.shape, weight[0], F32)
    w_copy = pltpu.make_async_remote_copy(
        src_ref=w_send, dst_ref=w_recv, send_sem=w_ssem, recv_sem=w_rsem,
        device_id={"replica": ahead}, device_id_type=MESH)
    w_copy.start()

    loads[0].wait()
    mine = cur.at[c]
    mine[...] = (b_v[...] / weight[0]).astype(BF16)
    cur_copy = pltpu.make_async_remote_copy(
        src_ref=mine, dst_ref=mine, send_sem=cur_ssem, recv_sem=cur_rsem,
        device_id={"shard": mate}, device_id_type=MESH)
    cur_copy.start()
    acc[...] = jnp.zeros(acc.shape, F32)
    bit = chips // 4
    while bit >= 1:
        for x in range(2 * bit, chips, 4 * bit):
            cot_copy(x).wait_recv()
        for x in range(bit, chips, 2 * bit):
            cot_copy(x).start()
        bit //= 2
    for k in range(early, min(look, last)):
        send_chunk(k)
    if look >= last:
        send_last()
    loads[1].wait()
    for x in range(1, chips, 2):
        cot_copy(x).wait_recv()
    cur_copy.wait_recv()
    w_copy.wait()
    w_send[...] = 0.5 * (w_send[...] + w_recv[...])
    w_store = pltpu.make_async_copy(w_send, w_out, w_ssem)
    w_store.start()

    contract = (((0,), (0,)), ((), ()))

    def arrived(k):
        for half in range(CORES):
            own_copy(k, half).wait()
        for j in range(len(peers)):
            for half in range(CORES):
                tok_copy(k, half, j).wait_recv()

    def partial_gradient(k, half):
        t = t_v[k, half].reshape(chips * own_tok, width)
        cots = c_v[...].reshape(chips * own_tok, kv)
        return lax.dot_general(t, cots, contract, preferred_element_type=F32)

    def product(k, t):
        here = pl.ds(pl.multiple_of(k * width, width), width)
        return (jnp.dot(t[0], cur[0, here, :], preferred_element_type=F32)
                + jnp.dot(t[1], cur[1, here, :], preferred_element_type=F32))

    def accumulate(k):
        made = product(k, [t_v[k, half].reshape(chips * own_tok, width) for half in range(CORES)])
        acc[...] += made.reshape(acc.shape)

    def send_sums(bit, t):
        part = pl.ds(t * block, block)
        for x in range(bit, chips, 2 * bit):
            p_send[x, t] = acc[flipped(z, x, chips), part, :].astype(BF16)
            p_copy(x, t).start()

    def add_sums(bit, t):
        part = pl.ds(t * block, block)
        for x in range(bit, chips, 2 * bit):
            p_copy(x, t).wait_recv()
            acc[flipped(z, x - bit, chips), part, :] += p_recv[x, t].astype(F32)

    bits = [1 << i for i in range(chips.bit_length() - 1)]

    def reduce_step(i, t):
        part = pl.ds(t * block, block)
        if i == 0:
            made = product(last, [
                t_v[last, half, :, part, :].reshape(chips * block, width) for half in range(CORES)])
            acc[:, part, :] += made.reshape(chips, block, kv)
        else:
            add_sums(bits[i - 1], t)
        if i < len(bits):
            send_sums(bits[i], t)
        else:
            p_send[0, t] = acc[z, part, :].astype(BF16)

    def send_gradient(k):
        gp_send[k] = partial_gradient(k, other).astype(BF16)
        gp_copy(k).start()
        g_v[k] = partial_gradient(k, c)

    def finish_gradient(k):
        here = pl.ds(pl.multiple_of(k * width, width), width)
        gp_copy(k).wait_recv()
        gradient = (g_v[k] + gp_recv[k].astype(F32)) / rep_tok
        velocity = MOMENT * m_v[here, :] + gradient
        m_v[here, :] = velocity
        stepped = b_v[here, :] - LEARN * (gradient + MOMENT * velocity)
        b_v[here, :] = stepped
        s_send[k] = stepped.astype(BF16)
        s_copy(k).start()
        store(k, 0).start()

    def mix(k):
        here = pl.ds(pl.multiple_of(k * width, width), width)
        s_copy(k).wait_recv()
        mixed = 0.5 * (b_v[here, :] + s_recv[k].astype(F32))
        b_v[here, :] = mixed
        deb_v[here, :] = mixed / w_send[0:1, 0:1]
        store(k, 1).start()
        store(k, 2).start()

    if nk > 1:
        @pl.loop(0, last)
        def _(k):
            arrived(k)

            @pl.when(k + look < last)
            def _():
                send_chunk(k + look)

            @pl.when(k + look == last)
            def _():
                send_last()

            send_gradient(k)
            accumulate(k)
            finish_gradient(k)

            @pl.when(k >= 2)
            def _():
                mix(k - 2)

    for half in range(CORES):
        own_copy(last, half).wait()
    for t in range(nt):
        for j in range(len(peers)):
            for half in range(CORES):
                end_copy(t, half, j).wait_recv()
        reduce_step(0, t)
        if t == nt - 1:
            send_gradient(last)
        for i in range(1, len(bits) + 1):
            if t >= i:
                reduce_step(i, t - i)
    finish_gradient(last)
    for k in range(max(0, nk - 3), last):
        mix(k)
    for late in range(nt, nt + len(bits)):
        for i in range(1, len(bits) + 1):
            if 0 <= late - i < nt:
                reduce_step(i, late - i)
    p_stores = [
        pltpu.make_async_copy(p_send.at[0, t], p_out.at[pl.ds(t * block, block), :], p_ssem.at[0, t])
        for t in range(nt)
    ]
    for p_store in p_stores:
        p_store.start()
    mix(last)

    for x in range(1, chips):
        cot_copy(x).wait_send()
        for t in range(nt):
            p_copy(x, t).wait_send()
    for j in range(len(peers)):
        for half in range(CORES):
            for k in range(last):
                tok_copy(k, half, j).wait_send()
            for t in range(nt):
                end_copy(t, half, j).wait_send()
    cur_copy.wait_send()
    for k in range(nk):
        gp_copy(k).wait_send()
        s_copy(k).wait_send()
        for i in range(3):
            store(k, i).wait()
    w_store.wait()
    for p_store in p_stores:
        p_store.wait()


def push_call(level, chips, tokens, cotangent, numer, moment, weight):
    own_tok, features = tokens.shape
    rows, kv = numer.shape
    nk = max(1, rows // 128)
    nt = max(1, own_tok // 32)
    block = own_tok // nt
    width = rows // nk
    n = chips - 1
    any_spec = pl.BlockSpec(memory_space=pl.ANY)
    dma = pltpu.SemaphoreType.DMA
    return pl.pallas_call(
        partial(push_kernel, 1 << level, chips, nk, 5),
        out_shape=(
            jax.ShapeDtypeStruct((own_tok, kv), BF16),
            jax.ShapeDtypeStruct((rows, kv), F32),
            jax.ShapeDtypeStruct((8, 128), F32),
            jax.ShapeDtypeStruct((rows, kv), F32),
            jax.ShapeDtypeStruct((rows, kv), F32),
        ),
        in_specs=[any_spec] * 4 + [pl.BlockSpec(memory_space=pltpu.SMEM)],
        out_specs=[any_spec] * 5,
        scratch_shapes=[
            pltpu.VMEM((nk, CORES, chips, own_tok, width), BF16),
            pltpu.VMEM((chips, own_tok, kv), BF16),
            pltpu.VMEM((rows, kv), F32),
            pltpu.VMEM((rows, kv), F32),
            pltpu.VMEM((CORES, rows, kv), BF16),
            pltpu.VMEM((chips, own_tok, kv), F32),
            pltpu.VMEM((chips, nt, block, kv), BF16),
            pltpu.VMEM((chips, nt, block, kv), BF16),
            pltpu.VMEM((nk, width, kv), BF16),
            pltpu.VMEM((nk, width, kv), BF16),
            pltpu.VMEM((nk, width, kv), F32),
            pltpu.VMEM((nk, width, kv), BF16),
            pltpu.VMEM((nk, width, kv), BF16),
            pltpu.VMEM((rows, kv), F32),
            pltpu.VMEM((8, 128), F32),
            pltpu.VMEM((8, 128), F32),
            dma((3,)), dma((nk, CORES)), dma((chips,)), dma((chips,)), dma((nk, CORES, n)), dma((nk, CORES, n)),
            dma((nt, CORES, n)), dma((nt, CORES, n)),
            dma(()), dma(()), dma((nk,)), dma((nk,)), dma((nk,)), dma((nk,)), dma((chips, nt)), dma((chips, nt)),
            dma(()), dma(()), dma((nk, 3)),
        ],
        compiler_params=pltpu.CompilerParams(
            collective_id=level, has_side_effects=True, vmem_limit_bytes=32 * 1024 * 1024),
        cost_estimate=pl.CostEstimate(
            flops=4 * own_tok * features * kv, bytes_accessed=12 * rows * kv, transcendentals=0),
        name=f"push_round_{level}",
    )(tokens, cotangent, numer, moment, weight)


def hand_out_kernel(p, mix, w, vel, deb, p_out, mix_out, w_out, vel_out, deb_out, w_v, sem):
    copies = [
        pltpu.make_async_copy(made, out, sem.at[i])
        for i, (made, out) in enumerate(((w, w_v), (mix, mix_out), (vel, vel_out), (deb, deb_out), (p, p_out)))
    ]
    for copy in copies:
        copy.start()
    copies[0].wait()
    w_out[0] = jnp.max(w_v[...])
    for copy in copies[1:]:
        copy.wait()


def hand_out(p, mix, w, vel, deb):
    any_spec = pl.BlockSpec(memory_space=pl.ANY)
    hbm = pl.BlockSpec(memory_space=pltpu.HBM)
    like = lambda a: jax.ShapeDtypeStruct(a.shape, a.dtype)
    return pl.pallas_call(
        hand_out_kernel,
        out_shape=(like(p), like(mix), jax.ShapeDtypeStruct((1,), F32), like(vel), like(deb)),
        in_specs=[any_spec] * 5,
        out_specs=[hbm, hbm, pl.BlockSpec(memory_space=pltpu.SMEM), hbm, hbm],
        scratch_shapes=[pltpu.VMEM((8, 128), F32), pltpu.SemaphoreType.DMA((5,))],
        cost_estimate=pl.CostEstimate(flops=0, bytes_accessed=12 * mix.size, transcendentals=0),
        name="hand_out",
    )(p, mix, w, vel, deb)


def shards(tokens, cotangent, biased, momentum, weight, round_index):
    hops = lax.axis_size("replica").bit_length() - 1
    chips = lax.axis_size("shard") // CORES
    power = round_index[0] % hops
    branches = [partial(push_call, level, chips) for level in range(hops)]
    made = lax.switch(power, branches, tokens, cotangent, biased[0], momentum[0], weight)
    output, mixed, weight_out, velocity, debiased = hand_out(*made)
    return (output, mixed[None], weight_out, velocity[None], debiased[None])


def solution(mesh):
    placed = (
        P(("replica", "shard"), None),
        P(("replica", "shard"), None),
        P("replica", "shard", None),
        P("replica", "shard", None),
        P("replica"),
        P(),
    )
    return jax.shard_map(
        shards,
        mesh=mesh,
        in_specs=placed,
        out_specs=(
            P(("replica", "shard"), None),
            P("replica", "shard", None),
            P("replica"),
            P("replica", "shard", None),
            P("replica", "shard", None),
        ),
        check_vma=False,
    )
```

```python
from functools import partial

import jax
import jax.numpy as jnp
from jax import lax
from jax.experimental import pallas as pl
from jax.experimental.pallas import tpu as pltpu
from jax.sharding import PartitionSpec as P

MOMENT = 0.9
LEARN = 0.5
MESH = pl.DeviceIdType.MESH
CORES = 2
BF16 = jnp.bfloat16
F32 = jnp.float32


def flipped(z, x, chips):
    total, bit = 0, 1
    while bit < chips:
        total = total + bit * ((z // bit + x // bit) % 2)
        bit *= 2
    return total


def partners(chips):
    order, bit = [], chips // 2
    while bit >= 1:
        order += list(range(bit, 2 * bit))
        bit //= 2
    return order


def push_kernel(dist, chips, nk, look, tok, cot, biased, momentum, weight,
                p_out, mix_out, w_out, vel_out, deb_out,
                tok_v, t_v, c_v, b_v, m_v, cur, acc, p_send, p_recv, gp_send, gp_recv, g_v, s_send, s_recv, deb_v,
                w_send, w_recv,
                load_sem, own_sem, c_ssem, c_rsem, t_ssem, t_rsem, e_ssem, e_rsem, cur_ssem, cur_rsem,
                gp_ssem, gp_rsem, s_ssem, s_rsem, p_ssem, p_rsem, w_ssem, w_rsem, store_sem):
    rows, kv = b_v.shape
    own_tok = tok.shape[0]
    width = rows // nk
    last = nk - 1
    nt, block = p_send.shape[1], p_send.shape[2]
    early = min(2, last)
    rep_tok = own_tok * chips * CORES
    replicas = lax.axis_size("replica")
    rep = lax.axis_index("replica")
    shard = lax.axis_index("shard")
    z = shard // CORES
    c = shard % CORES
    other = 1 - c
    mate = z * CORES + other
    ahead = (rep + dist) % replicas
    behind = (rep + replicas - dist) % replicas
    order = partners(chips)
    peers = [flipped(z, x, chips) for x in order]

    loads = [
        pltpu.make_async_copy(biased, b_v, load_sem.at[0]),
        pltpu.make_async_copy(momentum, m_v, load_sem.at[1]),
        pltpu.make_async_copy(cot, c_v.at[z], load_sem.at[2]),
        pltpu.make_async_copy(tok, tok_v, load_sem.at[3]),
    ]
    for load in loads[::-1]:
        load.start()

    def columns(chip, half, k):
        return pl.ds(pl.multiple_of((chip * CORES + half) * rows + k * width, width), width)

    def own_copy(k, half):
        return pltpu.make_async_copy(tok.at[:, columns(z, half, k)], t_v.at[k, half, z], own_sem.at[k, half])

    def tok_copy(k, half, j):
        return pltpu.make_async_remote_copy(
            src_ref=tok_v.at[:, columns(peers[j], half, k)], dst_ref=t_v.at[k, half, z],
            send_sem=t_ssem.at[k, half, j], recv_sem=t_rsem.at[k, half, j],
            device_id={"shard": peers[j] * CORES + c}, device_id_type=MESH)

    def end_copy(t, half, j):
        part = pl.ds(t * block, block)
        return pltpu.make_async_remote_copy(
            src_ref=tok_v.at[part, columns(peers[j], half, last)], dst_ref=t_v.at[last, half, z, part],
            send_sem=e_ssem.at[t, half, j], recv_sem=e_rsem.at[t, half, j],
            device_id={"shard": peers[j] * CORES + c}, device_id_type=MESH)

    def send_chunk(k):
        for j in range(len(peers)):
            for half in range(CORES):
                tok_copy(k, half, j).start()

    def send_last():
        for t in range(nt):
            for j in range(len(peers)):
                for half in range(CORES):
                    end_copy(t, half, j).start()

    def cot_copy(x):
        low = x & -x
        held = z if x == low else flipped(z, x - low, chips)
        return pltpu.make_async_remote_copy(
            src_ref=c_v.at[held], dst_ref=c_v.at[held], send_sem=c_ssem.at[x], recv_sem=c_rsem.at[x],
            device_id={"shard": flipped(z, low, chips) * CORES + c}, device_id_type=MESH)

    def p_copy(x, t):
        return pltpu.make_async_remote_copy(
            src_ref=p_send.at[x, t], dst_ref=p_recv.at[x, t], send_sem=p_ssem.at[x, t], recv_sem=p_rsem.at[x, t],
            device_id={"shard": flipped(z, x & -x, chips) * CORES + c}, device_id_type=MESH)

    def gp_copy(k):
        return pltpu.make_async_remote_copy(
            src_ref=gp_send.at[k], dst_ref=gp_recv.at[k], send_sem=gp_ssem.at[k], recv_sem=gp_rsem.at[k],
            device_id={"shard": mate}, device_id_type=MESH)

    def s_copy(k):
        return pltpu.make_async_remote_copy(
            src_ref=s_send.at[k], dst_ref=s_recv.at[k],
            send_sem=s_ssem.at[k], recv_sem=s_rsem.at[k],
            device_id={"replica": ahead}, device_id_type=MESH)

    def store(k, i):
        here = pl.ds(pl.multiple_of(k * width, width), width)
        made, out = ((m_v, vel_out), (b_v, mix_out), (deb_v, deb_out))[i]
        return pltpu.make_async_copy(made.at[here, :], out.at[here, :], store_sem.at[k, i])

    for k in range(nk):
        for half in range(CORES):
            own_copy(k, half).start()

    barrier = pltpu.get_barrier_semaphore()
    for peer in peers:
        pl.semaphore_signal(barrier, inc=1, device_id={"shard": peer * CORES + c}, device_id_type=MESH)
    pl.semaphore_signal(barrier, inc=1, device_id={"shard": mate}, device_id_type=MESH)
    pl.semaphore_signal(barrier, inc=1, device_id={"replica": behind}, device_id_type=MESH)
    pl.semaphore_wait(barrier, len(peers) + 2)

    loads[2].wait()
    cot_copy(chips // 2).start()
    loads[3].wait()
    for k in range(early):
        send_chunk(k)

    w_send[...] = jnp.full(w_send.shape, weight[0], F32)
    w_copy = pltpu.make_async_remote_copy(
        src_ref=w_send, dst_ref=w_recv, send_sem=w_ssem, recv_sem=w_rsem,
        device_id={"replica": ahead}, device_id_type=MESH)
    w_copy.start()

    loads[0].wait()
    mine = cur.at[c]
    mine[...] = (b_v[...] / weight[0]).astype(BF16)
    cur_copy = pltpu.make_async_remote_copy(
        src_ref=mine, dst_ref=mine, send_sem=cur_ssem, recv_sem=cur_rsem,
        device_id={"shard": mate}, device_id_type=MESH)
    cur_copy.start()
    acc[...] = jnp.zeros(acc.shape, F32)
    bit = chips // 4
    while bit >= 1:
        for x in range(2 * bit, chips, 4 * bit):
            cot_copy(x).wait_recv()
        for x in range(bit, chips, 2 * bit):
            cot_copy(x).start()
        bit //= 2
    for k in range(early, min(look, last)):
        send_chunk(k)
    if look >= last:
        send_last()
    loads[1].wait()
    for x in range(1, chips, 2):
        cot_copy(x).wait_recv()
    cur_copy.wait_recv()
    w_copy.wait()
    w_send[...] = 0.5 * (w_send[...] + w_recv[...])
    w_store = pltpu.make_async_copy(w_send, w_out, w_ssem)
    w_store.start()

    contract = (((0,), (0,)), ((), ()))

    def arrived(k):
        for half in range(CORES):
            own_copy(k, half).wait()
        for j in range(len(peers)):
            for half in range(CORES):
                tok_copy(k, half, j).wait_recv()

    def partial_gradient(k, half):
        t = t_v[k, half].reshape(chips * own_tok, width)
        cots = c_v[...].reshape(chips * own_tok, kv)
        return lax.dot_general(t, cots, contract, preferred_element_type=F32)

    def product(k, t):
        here = pl.ds(pl.multiple_of(k * width, width), width)
        return (jnp.dot(t[0], cur[0, here, :], preferred_element_type=F32)
                + jnp.dot(t[1], cur[1, here, :], preferred_element_type=F32))

    def accumulate(k):
        made = product(k, [t_v[k, half].reshape(chips * own_tok, width) for half in range(CORES)])
        acc[...] += made.reshape(acc.shape)

    def send_sums(bit, t):
        part = pl.ds(t * block, block)
        for x in range(bit, chips, 2 * bit):
            p_send[x, t] = acc[flipped(z, x, chips), part, :].astype(BF16)
            p_copy(x, t).start()

    def add_sums(bit, t):
        part = pl.ds(t * block, block)
        for x in range(bit, chips, 2 * bit):
            p_copy(x, t).wait_recv()
            acc[flipped(z, x - bit, chips), part, :] += p_recv[x, t].astype(F32)

    bits = [1 << i for i in range(chips.bit_length() - 1)]

    def reduce_step(i, t):
        part = pl.ds(t * block, block)
        if i == 0:
            made = product(last, [
                t_v[last, half, :, part, :].reshape(chips * block, width) for half in range(CORES)])
            acc[:, part, :] += made.reshape(chips, block, kv)
        else:
            add_sums(bits[i - 1], t)
        if i < len(bits):
            send_sums(bits[i], t)
        else:
            p_send[0, t] = acc[z, part, :].astype(BF16)

    def send_gradient(k):
        gp_send[k] = partial_gradient(k, other).astype(BF16)
        gp_copy(k).start()
        g_v[k] = partial_gradient(k, c)

    def finish_gradient(k):
        here = pl.ds(pl.multiple_of(k * width, width), width)
        gp_copy(k).wait_recv()
        gradient = (g_v[k] + gp_recv[k].astype(F32)) / rep_tok
        velocity = MOMENT * m_v[here, :] + gradient
        m_v[here, :] = velocity
        stepped = b_v[here, :] - LEARN * (gradient + MOMENT * velocity)
        b_v[here, :] = stepped
        s_send[k] = stepped.astype(BF16)
        s_copy(k).start()
        store(k, 0).start()

    def mix(k):
        here = pl.ds(pl.multiple_of(k * width, width), width)
        s_copy(k).wait_recv()
        mixed = 0.5 * (b_v[here, :] + s_recv[k].astype(F32))
        b_v[here, :] = mixed
        deb_v[here, :] = mixed / w_send[0:1, 0:1]
        store(k, 1).start()
        store(k, 2).start()

    if nk > 1:
        @pl.loop(0, last)
        def _(k):
            arrived(k)

            @pl.when(k + look < last)
            def _():
                send_chunk(k + look)

            @pl.when(k + look == last)
            def _():
                send_last()

            send_gradient(k)
            accumulate(k)
            finish_gradient(k)

            @pl.when(k >= 2)
            def _():
                mix(k - 2)

    for half in range(CORES):
        own_copy(last, half).wait()
    for t in range(nt):
        for j in range(len(peers)):
            for half in range(CORES):
                end_copy(t, half, j).wait_recv()
        reduce_step(0, t)
        if t == nt - 1:
            send_gradient(last)
        for i in range(1, len(bits) + 1):
            if t >= i:
                reduce_step(i, t - i)
    finish_gradient(last)
    for k in range(max(0, nk - 3), last):
        mix(k)
    for late in range(nt, nt + len(bits)):
        for i in range(1, len(bits) + 1):
            if 0 <= late - i < nt:
                reduce_step(i, late - i)
    p_stores = [
        pltpu.make_async_copy(p_send.at[0, t], p_out.at[pl.ds(t * block, block), :], p_ssem.at[0, t])
        for t in range(nt)
    ]
    for p_store in p_stores:
        p_store.start()
    mix(last)

    for x in range(1, chips):
        cot_copy(x).wait_send()
        for t in range(nt):
            p_copy(x, t).wait_send()
    for j in range(len(peers)):
        for half in range(CORES):
            for k in range(last):
                tok_copy(k, half, j).wait_send()
            for t in range(nt):
                end_copy(t, half, j).wait_send()
    cur_copy.wait_send()
    for k in range(nk):
        gp_copy(k).wait_send()
        s_copy(k).wait_send()
        for i in range(3):
            store(k, i).wait()
    w_store.wait()
    for p_store in p_stores:
        p_store.wait()


def push_call(level, chips, tokens, cotangent, numer, moment, weight):
    own_tok, features = tokens.shape
    rows, kv = numer.shape
    nk = max(1, rows // 128)
    nt = max(1, own_tok // 32)
    block = own_tok // nt
    width = rows // nk
    n = chips - 1
    any_spec = pl.BlockSpec(memory_space=pl.ANY)
    dma = pltpu.SemaphoreType.DMA
    return pl.pallas_call(
        partial(push_kernel, 1 << level, chips, nk, 5),
        out_shape=(
            jax.ShapeDtypeStruct((own_tok, kv), BF16),
            jax.ShapeDtypeStruct((rows, kv), F32),
            jax.ShapeDtypeStruct((8, 128), F32),
            jax.ShapeDtypeStruct((rows, kv), F32),
            jax.ShapeDtypeStruct((rows, kv), F32),
        ),
        in_specs=[any_spec] * 4 + [pl.BlockSpec(memory_space=pltpu.SMEM)],
        out_specs=[any_spec] * 5,
        scratch_shapes=[
            pltpu.VMEM((own_tok, features), BF16),
            pltpu.VMEM((nk, CORES, chips, own_tok, width), BF16),
            pltpu.VMEM((chips, own_tok, kv), BF16),
            pltpu.VMEM((rows, kv), F32),
            pltpu.VMEM((rows, kv), F32),
            pltpu.VMEM((CORES, rows, kv), BF16),
            pltpu.VMEM((chips, own_tok, kv), F32),
            pltpu.VMEM((chips, nt, block, kv), BF16),
            pltpu.VMEM((chips, nt, block, kv), BF16),
            pltpu.VMEM((nk, width, kv), BF16),
            pltpu.VMEM((nk, width, kv), BF16),
            pltpu.VMEM((nk, width, kv), F32),
            pltpu.VMEM((nk, width, kv), BF16),
            pltpu.VMEM((nk, width, kv), BF16),
            pltpu.VMEM((rows, kv), F32),
            pltpu.VMEM((8, 128), F32),
            pltpu.VMEM((8, 128), F32),
            dma((4,)), dma((nk, CORES)), dma((chips,)), dma((chips,)), dma((nk, CORES, n)), dma((nk, CORES, n)),
            dma((nt, CORES, n)), dma((nt, CORES, n)),
            dma(()), dma(()), dma((nk,)), dma((nk,)), dma((nk,)), dma((nk,)), dma((chips, nt)), dma((chips, nt)),
            dma(()), dma(()), dma((nk, 3)),
        ],
        compiler_params=pltpu.CompilerParams(
            collective_id=level, has_side_effects=True, vmem_limit_bytes=32 * 1024 * 1024),
        cost_estimate=pl.CostEstimate(
            flops=4 * own_tok * features * kv, bytes_accessed=12 * rows * kv, transcendentals=0),
        name=f"push_round_{level}",
    )(tokens, cotangent, numer, moment, weight)


def hand_out_kernel(p, mix, w, vel, deb, p_out, mix_out, w_out, vel_out, deb_out, w_v, sem):
    copies = [
        pltpu.make_async_copy(made, out, sem.at[i])
        for i, (made, out) in enumerate(((w, w_v), (mix, mix_out), (vel, vel_out), (deb, deb_out), (p, p_out)))
    ]
    for copy in copies:
        copy.start()
    copies[0].wait()
    w_out[0] = jnp.max(w_v[...])
    for copy in copies[1:]:
        copy.wait()


def hand_out(p, mix, w, vel, deb):
    any_spec = pl.BlockSpec(memory_space=pl.ANY)
    hbm = pl.BlockSpec(memory_space=pltpu.HBM)
    like = lambda a: jax.ShapeDtypeStruct(a.shape, a.dtype)
    return pl.pallas_call(
        hand_out_kernel,
        out_shape=(like(p), like(mix), jax.ShapeDtypeStruct((1,), F32), like(vel), like(deb)),
        in_specs=[any_spec] * 5,
        out_specs=[hbm, hbm, pl.BlockSpec(memory_space=pltpu.SMEM), hbm, hbm],
        scratch_shapes=[pltpu.VMEM((8, 128), F32), pltpu.SemaphoreType.DMA((5,))],
        compiler_params=pltpu.CompilerParams(vmem_limit_bytes=1024 * 1024),
        cost_estimate=pl.CostEstimate(flops=0, bytes_accessed=12 * mix.size, transcendentals=0),
        name="hand_out",
    )(p, mix, w, vel, deb)


def shards(tokens, cotangent, biased, momentum, weight, round_index):
    hops = lax.axis_size("replica").bit_length() - 1
    chips = lax.axis_size("shard") // CORES
    power = round_index[0] % hops
    branches = [partial(push_call, level, chips) for level in range(hops)]
    made = lax.switch(power, branches, tokens, cotangent, biased[0], momentum[0], weight)
    output, mixed, weight_out, velocity, debiased = hand_out(*made)
    return (output, mixed[None], weight_out, velocity[None], debiased[None])


def solution(mesh):
    placed = (
        P(("replica", "shard"), None),
        P(("replica", "shard"), None),
        P("replica", "shard", None),
        P("replica", "shard", None),
        P("replica"),
        P(),
    )
    return jax.shard_map(
        shards,
        mesh=mesh,
        in_specs=placed,
        out_specs=(
            P(("replica", "shard"), None),
            P("replica", "shard", None),
            P("replica"),
            P("replica", "shard", None),
            P("replica", "shard", None),
        ),
        check_vma=False,
    )
```

```python
from functools import partial

import jax
import jax.numpy as jnp
from jax import lax
from jax.experimental import pallas as pl
from jax.experimental.pallas import tpu as pltpu
from jax.sharding import PartitionSpec as P

MOMENT = 0.9
LEARN = 0.5
MESH = pl.DeviceIdType.MESH
CORES = 2
BF16 = jnp.bfloat16
F32 = jnp.float32


def flipped(z, x, chips):
    total, bit = 0, 1
    while bit < chips:
        total = total + bit * ((z // bit + x // bit) % 2)
        bit *= 2
    return total


def partners(chips):
    order, bit = [], chips // 2
    while bit >= 1:
        order += list(range(bit, 2 * bit))
        bit //= 2
    return order


def push_kernel(dist, chips, nk, look, tok, cot, biased, momentum, weight,
                p_out, mix_out, w_out, vel_out,
                tok_v, t_v, c_v, b_v, m_v, cur, acc, p_send, p_recv, gp_send, gp_recv, g_v, s_send, s_recv,
                w_send, w_recv,
                load_sem, own_sem, c_ssem, c_rsem, t_ssem, t_rsem, e_ssem, e_rsem, cur_ssem, cur_rsem,
                gp_ssem, gp_rsem, s_ssem, s_rsem, p_ssem, p_rsem, w_ssem, w_rsem, store_sem):
    rows, kv = b_v.shape
    own_tok = tok.shape[0]
    width = rows // nk
    last = nk - 1
    nt, block = p_send.shape[1], p_send.shape[2]
    early = min(2, last)
    rep_tok = own_tok * chips * CORES
    replicas = lax.axis_size("replica")
    rep = lax.axis_index("replica")
    shard = lax.axis_index("shard")
    z = shard // CORES
    c = shard % CORES
    other = 1 - c
    mate = z * CORES + other
    ahead = (rep + dist) % replicas
    behind = (rep + replicas - dist) % replicas
    order = partners(chips)
    peers = [flipped(z, x, chips) for x in order]

    loads = [
        pltpu.make_async_copy(biased, b_v, load_sem.at[0]),
        pltpu.make_async_copy(momentum, m_v, load_sem.at[1]),
        pltpu.make_async_copy(cot, c_v.at[z], load_sem.at[2]),
        pltpu.make_async_copy(tok, tok_v, load_sem.at[3]),
    ]
    for load in loads[::-1]:
        load.start()

    def columns(chip, half, k):
        return pl.ds(pl.multiple_of((chip * CORES + half) * rows + k * width, width), width)

    def own_copy(k, half):
        return pltpu.make_async_copy(tok.at[:, columns(z, half, k)], t_v.at[k, half, z], own_sem.at[k, half])

    def tok_copy(k, half, j):
        return pltpu.make_async_remote_copy(
            src_ref=tok_v.at[:, columns(peers[j], half, k)], dst_ref=t_v.at[k, half, z],
            send_sem=t_ssem.at[k, half, j], recv_sem=t_rsem.at[k, half, j],
            device_id={"shard": peers[j] * CORES + c}, device_id_type=MESH)

    def end_copy(t, half, j):
        part = pl.ds(t * block, block)
        return pltpu.make_async_remote_copy(
            src_ref=tok_v.at[part, columns(peers[j], half, last)], dst_ref=t_v.at[last, half, z, part],
            send_sem=e_ssem.at[t, half, j], recv_sem=e_rsem.at[t, half, j],
            device_id={"shard": peers[j] * CORES + c}, device_id_type=MESH)

    def send_chunk(k):
        for j in range(len(peers)):
            for half in range(CORES):
                tok_copy(k, half, j).start()

    def send_last():
        for t in range(nt):
            for j in range(len(peers)):
                for half in range(CORES):
                    end_copy(t, half, j).start()

    def cot_copy(x):
        low = x & -x
        held = z if x == low else flipped(z, x - low, chips)
        return pltpu.make_async_remote_copy(
            src_ref=c_v.at[held], dst_ref=c_v.at[held], send_sem=c_ssem.at[x], recv_sem=c_rsem.at[x],
            device_id={"shard": flipped(z, low, chips) * CORES + c}, device_id_type=MESH)

    def p_copy(x, t):
        return pltpu.make_async_remote_copy(
            src_ref=p_send.at[x, t], dst_ref=p_recv.at[x, t], send_sem=p_ssem.at[x, t], recv_sem=p_rsem.at[x, t],
            device_id={"shard": flipped(z, x & -x, chips) * CORES + c}, device_id_type=MESH)

    def gp_copy(k):
        return pltpu.make_async_remote_copy(
            src_ref=gp_send.at[k], dst_ref=gp_recv.at[k], send_sem=gp_ssem.at[k], recv_sem=gp_rsem.at[k],
            device_id={"shard": mate}, device_id_type=MESH)

    def s_copy(k):
        return pltpu.make_async_remote_copy(
            src_ref=s_send.at[k], dst_ref=s_recv.at[k],
            send_sem=s_ssem.at[k], recv_sem=s_rsem.at[k],
            device_id={"replica": ahead}, device_id_type=MESH)

    def store(k, i):
        here = pl.ds(pl.multiple_of(k * width, width), width)
        made, out = ((m_v, vel_out), (b_v, mix_out))[i]
        return pltpu.make_async_copy(made.at[here, :], out.at[here, :], store_sem.at[k, i])

    for k in range(nk):
        for half in range(CORES):
            own_copy(k, half).start()

    mine = cur.at[c]
    barrier = pltpu.get_barrier_semaphore()
    for peer in peers:
        pl.semaphore_signal(barrier, inc=1, device_id={"shard": peer * CORES + c}, device_id_type=MESH)
    pl.semaphore_signal(barrier, inc=1, device_id={"shard": mate}, device_id_type=MESH)
    pl.semaphore_signal(barrier, inc=1, device_id={"replica": behind}, device_id_type=MESH)
    loads[0].wait()
    mine[...] = (b_v[...] / weight[0]).astype(BF16)
    acc[...] = jnp.zeros(acc.shape, F32)
    pl.semaphore_wait(barrier, len(peers) + 2)

    loads[2].wait()
    cot_copy(chips // 2).start()
    loads[3].wait()
    for k in range(min(1, last)):
        send_chunk(k)

    w_send[...] = jnp.full(w_send.shape, weight[0], F32)
    w_copy = pltpu.make_async_remote_copy(
        src_ref=w_send, dst_ref=w_recv, send_sem=w_ssem, recv_sem=w_rsem,
        device_id={"replica": ahead}, device_id_type=MESH)
    w_copy.start()

    cur_copy = pltpu.make_async_remote_copy(
        src_ref=mine, dst_ref=mine, send_sem=cur_ssem, recv_sem=cur_rsem,
        device_id={"shard": mate}, device_id_type=MESH)
    cur_copy.start()
    for k in range(min(1, last), early):
        send_chunk(k)
    bit = chips // 4
    while bit >= 1:
        for x in range(2 * bit, chips, 4 * bit):
            cot_copy(x).wait_recv()
        for x in range(bit, chips, 2 * bit):
            cot_copy(x).start()
        bit //= 2
    for k in range(early, min(look, last)):
        send_chunk(k)
    if look >= last:
        send_last()
    loads[1].wait()
    for x in range(1, chips, 2):
        cot_copy(x).wait_recv()
    cur_copy.wait_recv()
    w_copy.wait()
    w_send[...] = 0.5 * (w_send[...] + w_recv[...])
    w_store = pltpu.make_async_copy(w_send, w_out, w_ssem)
    w_store.start()

    contract = (((0,), (0,)), ((), ()))

    def arrived(k):
        for half in range(CORES):
            own_copy(k, half).wait()
        for j in range(len(peers)):
            for half in range(CORES):
                tok_copy(k, half, j).wait_recv()

    def partial_gradient(k, half):
        t = t_v[k, half].reshape(chips * own_tok, width)
        cots = c_v[...].reshape(chips * own_tok, kv)
        return lax.dot_general(t, cots, contract, preferred_element_type=F32)

    def product(k, t):
        here = pl.ds(pl.multiple_of(k * width, width), width)
        return (jnp.dot(t[0], cur[0, here, :], preferred_element_type=F32)
                + jnp.dot(t[1], cur[1, here, :], preferred_element_type=F32))

    def accumulate(k):
        made = product(k, [t_v[k, half].reshape(chips * own_tok, width) for half in range(CORES)])
        acc[...] += made.reshape(acc.shape)

    def send_sums(bit, t):
        part = pl.ds(t * block, block)
        for x in range(bit, chips, 2 * bit):
            p_send[x, t] = acc[flipped(z, x, chips), part, :].astype(BF16)
            p_copy(x, t).start()

    def add_sums(bit, t):
        part = pl.ds(t * block, block)
        for x in range(bit, chips, 2 * bit):
            p_copy(x, t).wait_recv()
            acc[flipped(z, x - bit, chips), part, :] += p_recv[x, t].astype(F32)

    bits = [1 << i for i in range(chips.bit_length() - 1)]

    def reduce_step(i, t):
        part = pl.ds(t * block, block)
        if i == 0:
            made = product(last, [
                t_v[last, half, :, part, :].reshape(chips * block, width) for half in range(CORES)])
            acc[:, part, :] += made.reshape(chips, block, kv)
        else:
            add_sums(bits[i - 1], t)
        if i < len(bits):
            send_sums(bits[i], t)
        else:
            p_send[0, t] = acc[z, part, :].astype(BF16)

    def send_gradient(k):
        gp_send[k] = partial_gradient(k, other).astype(BF16)
        gp_copy(k).start()

    def finish_gradient(k):
        here = pl.ds(pl.multiple_of(k * width, width), width)
        gp_copy(k).wait_recv()
        gradient = (g_v[k] + gp_recv[k].astype(F32)) / rep_tok
        velocity = MOMENT * m_v[here, :] + gradient
        m_v[here, :] = velocity
        stepped = b_v[here, :] - LEARN * (gradient + MOMENT * velocity)
        b_v[here, :] = stepped
        s_send[k] = stepped.astype(BF16)
        s_copy(k).start()
        store(k, 0).start()

    def mix(k):
        here = pl.ds(pl.multiple_of(k * width, width), width)
        s_copy(k).wait_recv()
        b_v[here, :] = 0.5 * (b_v[here, :] + s_recv[k].astype(F32))
        store(k, 1).start()

    if nk > 1:
        @pl.loop(0, last)
        def _(k):
            arrived(k)
            send_gradient(k)

            @pl.when(k + look < last)
            def _():
                send_chunk(k + look)

            @pl.when(k + look == last)
            def _():
                send_last()

            g_v[k] = partial_gradient(k, c)
            accumulate(k)

            @pl.when(k >= 1)
            def _():
                finish_gradient(k - 1)

            @pl.when(k >= 4)
            def _():
                mix(k - 4)

    for half in range(CORES):
        own_copy(last, half).wait()
    for t in range(nt):
        for j in range(len(peers)):
            for half in range(CORES):
                end_copy(t, half, j).wait_recv()
        reduce_step(0, t)
        if t == nt - 1:
            send_gradient(last)
            if last >= 1:
                finish_gradient(last - 1)
            g_v[last] = partial_gradient(last, c)
        for i in range(1, len(bits) + 1):
            if t >= i:
                reduce_step(i, t - i)
    finish_gradient(last)
    for k in range(max(0, last - 4), last):
        mix(k)
    for late in range(nt, nt + len(bits)):
        for i in range(1, len(bits) + 1):
            if 0 <= late - i < nt:
                reduce_step(i, late - i)
    p_stores = [
        pltpu.make_async_copy(p_send.at[0, t], p_out.at[pl.ds(t * block, block), :], p_ssem.at[0, t])
        for t in range(nt)
    ]
    for p_store in p_stores:
        p_store.start()
    mix(last)

    for x in range(1, chips):
        cot_copy(x).wait_send()
        for t in range(nt):
            p_copy(x, t).wait_send()
    for j in range(len(peers)):
        for half in range(CORES):
            for k in range(last):
                tok_copy(k, half, j).wait_send()
            for t in range(nt):
                end_copy(t, half, j).wait_send()
    cur_copy.wait_send()
    for k in range(nk):
        gp_copy(k).wait_send()
        s_copy(k).wait_send()
        for i in range(2):
            store(k, i).wait()
    w_store.wait()
    for p_store in p_stores:
        p_store.wait()


def push_call(level, chips, tokens, cotangent, numer, moment, weight):
    own_tok, features = tokens.shape
    rows, kv = numer.shape
    nk = max(1, rows // 128)
    nt = max(1, own_tok // 32)
    block = own_tok // nt
    width = rows // nk
    n = chips - 1
    any_spec = pl.BlockSpec(memory_space=pl.ANY)
    dma = pltpu.SemaphoreType.DMA
    return pl.pallas_call(
        partial(push_kernel, 1 << level, chips, nk, 2),
        out_shape=(
            jax.ShapeDtypeStruct((own_tok, kv), BF16),
            jax.ShapeDtypeStruct((rows, kv), F32),
            jax.ShapeDtypeStruct((8, 128), F32),
            jax.ShapeDtypeStruct((rows, kv), F32),
        ),
        in_specs=[any_spec] * 4 + [pl.BlockSpec(memory_space=pltpu.SMEM)],
        out_specs=[any_spec] * 4,
        scratch_shapes=[
            pltpu.VMEM((own_tok, features), BF16),
            pltpu.VMEM((nk, CORES, chips, own_tok, width), BF16),
            pltpu.VMEM((chips, own_tok, kv), BF16),
            pltpu.VMEM((rows, kv), F32),
            pltpu.VMEM((rows, kv), F32),
            pltpu.VMEM((CORES, rows, kv), BF16),
            pltpu.VMEM((chips, own_tok, kv), F32),
            pltpu.VMEM((chips, nt, block, kv), BF16),
            pltpu.VMEM((chips, nt, block, kv), BF16),
            pltpu.VMEM((nk, width, kv), BF16),
            pltpu.VMEM((nk, width, kv), BF16),
            pltpu.VMEM((nk, width, kv), F32),
            pltpu.VMEM((nk, width, kv), BF16),
            pltpu.VMEM((nk, width, kv), BF16),
            pltpu.VMEM((8, 128), F32),
            pltpu.VMEM((8, 128), F32),
            dma((4,)), dma((nk, CORES)), dma((chips,)), dma((chips,)), dma((nk, CORES, n)), dma((nk, CORES, n)),
            dma((nt, CORES, n)), dma((nt, CORES, n)),
            dma(()), dma(()), dma((nk,)), dma((nk,)), dma((nk,)), dma((nk,)), dma((chips, nt)), dma((chips, nt)),
            dma(()), dma(()), dma((nk, 2)),
        ],
        compiler_params=pltpu.CompilerParams(
            collective_id=level, has_side_effects=True, vmem_limit_bytes=32 * 1024 * 1024),
        cost_estimate=pl.CostEstimate(
            flops=4 * own_tok * features * kv, bytes_accessed=12 * rows * kv, transcendentals=0),
        name=f"push_round_{level}",
    )(tokens, cotangent, numer, moment, weight)


def hand_out_kernel(parts, p, mix, w, vel, p_out, mix_out, w_out, vel_out, deb_out,
                    p_v, mix_v, w_v, vel_v, deb_v, in_sem, out_sem, small_sem):
    size = mix_v.shape[0] // parts

    def load(i, which):
        here = pl.ds(i * size, size)
        made, held = ((mix, mix_v), (vel, vel_v))[which]
        return pltpu.make_async_copy(made.at[here, :], held.at[here, :], in_sem.at[i, which])

    def store(i, which):
        here = pl.ds(i * size, size)
        held, out = ((mix_v, mix_out), (vel_v, vel_out), (deb_v, deb_out))[which]
        return pltpu.make_async_copy(held.at[here, :], out.at[here, :], out_sem.at[i, which])

    w_load = pltpu.make_async_copy(w, w_v, small_sem.at[0])
    p_load = pltpu.make_async_copy(p, p_v, small_sem.at[1])
    p_store = pltpu.make_async_copy(p_v, p_out, small_sem.at[2])
    w_load.start()
    for i in range(parts):
        load(i, 0).start()
        load(i, 1).start()
    p_load.start()
    w_load.wait()
    scale = w_v[0:1, 0:1]
    w_out[0] = jnp.max(w_v[...])
    for i in range(parts):
        here = pl.ds(i * size, size)
        load(i, 0).wait()
        store(i, 0).start()
        deb_v[here, :] = mix_v[here, :] / scale
        store(i, 2).start()
        load(i, 1).wait()
        store(i, 1).start()
    p_load.wait()
    p_store.start()
    for i in range(parts):
        for which in range(3):
            store(i, which).wait()
    p_store.wait()


def hand_out(p, mix, w, vel):
    any_spec = pl.BlockSpec(memory_space=pl.ANY)
    hbm = pl.BlockSpec(memory_space=pltpu.HBM)
    like = lambda a: jax.ShapeDtypeStruct(a.shape, a.dtype)
    held = lambda a: pltpu.VMEM(a.shape, a.dtype)
    parts = max(1, mix.shape[0] // 128)
    dma = pltpu.SemaphoreType.DMA
    return pl.pallas_call(
        partial(hand_out_kernel, parts),
        out_shape=(like(p), like(mix), jax.ShapeDtypeStruct((1,), F32), like(vel), like(mix)),
        in_specs=[any_spec] * 4,
        out_specs=[hbm, hbm, pl.BlockSpec(memory_space=pltpu.SMEM), hbm, hbm],
        scratch_shapes=[held(p), held(mix), held(w), held(vel), held(mix),
                        dma((parts, 2)), dma((parts, 3)), dma((3,))],
        compiler_params=pltpu.CompilerParams(vmem_limit_bytes=8 * 1024 * 1024),
        cost_estimate=pl.CostEstimate(flops=0, bytes_accessed=12 * mix.size, transcendentals=0),
        name="hand_out",
    )(p, mix, w, vel)


def shards(tokens, cotangent, biased, momentum, weight, round_index):
    hops = lax.axis_size("replica").bit_length() - 1
    chips = lax.axis_size("shard") // CORES
    power = round_index[0] % hops
    branches = [partial(push_call, level, chips) for level in range(hops)]
    made = lax.switch(power, branches, tokens, cotangent, biased[0], momentum[0], weight)
    output, mixed, weight_out, velocity, debiased = hand_out(*made)
    return (output, mixed[None], weight_out, velocity[None], debiased[None])


def solution(mesh):
    placed = (
        P(("replica", "shard"), None),
        P(("replica", "shard"), None),
        P("replica", "shard", None),
        P("replica", "shard", None),
        P("replica"),
        P(),
    )
    return jax.shard_map(
        shards,
        mesh=mesh,
        in_specs=placed,
        out_specs=(
            P(("replica", "shard"), None),
            P("replica", "shard", None),
            P("replica"),
            P("replica", "shard", None),
            P("replica", "shard", None),
        ),
        check_vma=False,
    )
```

```python
from functools import partial

import jax
import jax.numpy as jnp
from jax import lax
from jax.experimental import pallas as pl
from jax.experimental.pallas import tpu as pltpu
from jax.sharding import PartitionSpec as P

MOMENT = 0.9
LEARN = 0.5
MESH = pl.DeviceIdType.MESH
CORES = 1
BF16 = jnp.bfloat16
F32 = jnp.float32


def flipped(z, x, chips):
    total, bit = 0, 1
    while bit < chips:
        total = total + bit * ((z // bit + x // bit) % 2)
        bit *= 2
    return total


def partners(chips):
    order, bit = [], chips // 2
    while bit >= 1:
        order += list(range(bit, 2 * bit))
        bit //= 2
    return order


def push_kernel(dist, chips, nk, look, tok, cot, biased, momentum, weight,
                p_out, mix_out, w_out, vel_out,
                tok_v, t_v, c_v, b_v, m_v, cur, acc, p_send, p_recv, s_send, s_recv,
                w_send, w_recv,
                load_sem, own_sem, c_ssem, c_rsem, t_ssem, t_rsem, e_ssem, e_rsem, s_ssem, s_rsem, p_ssem, p_rsem, w_ssem, w_rsem, store_sem):
    rows, kv = b_v.shape
    own_tok = tok.shape[0]
    width = rows // nk
    last = nk - 1
    nt, block = p_send.shape[1], p_send.shape[2]
    early = min(2, last)
    rep_tok = own_tok * chips * CORES
    replicas = lax.axis_size("replica")
    rep = lax.axis_index("replica")
    shard = lax.axis_index("shard")
    z = shard // CORES
    c = shard % CORES
    ahead = (rep + dist) % replicas
    behind = (rep + replicas - dist) % replicas
    order = partners(chips)
    peers = [flipped(z, x, chips) for x in order]

    loads = [
        pltpu.make_async_copy(biased, b_v, load_sem.at[0]),
        pltpu.make_async_copy(momentum, m_v, load_sem.at[1]),
        pltpu.make_async_copy(cot, c_v.at[z], load_sem.at[2]),
        pltpu.make_async_copy(tok, tok_v, load_sem.at[3]),
    ]
    for load in loads[::-1]:
        load.start()

    def columns(chip, half, k):
        return pl.ds(pl.multiple_of((chip * CORES + half) * rows + k * width, width), width)

    def own_copy(k, half):
        return pltpu.make_async_copy(tok.at[:, columns(z, half, k)], t_v.at[k, half, z], own_sem.at[k, half])

    def tok_copy(k, half, j):
        return pltpu.make_async_remote_copy(
            src_ref=tok_v.at[:, columns(peers[j], half, k)], dst_ref=t_v.at[k, half, z],
            send_sem=t_ssem.at[k, half, j], recv_sem=t_rsem.at[k, half, j],
            device_id={"shard": peers[j] * CORES + c}, device_id_type=MESH)

    def end_copy(t, half, j):
        part = pl.ds(t * block, block)
        return pltpu.make_async_remote_copy(
            src_ref=tok_v.at[part, columns(peers[j], half, last)], dst_ref=t_v.at[last, half, z, part],
            send_sem=e_ssem.at[t, half, j], recv_sem=e_rsem.at[t, half, j],
            device_id={"shard": peers[j] * CORES + c}, device_id_type=MESH)

    def send_chunk(k):
        for j in range(len(peers)):
            for half in range(CORES):
                tok_copy(k, half, j).start()

    def send_last():
        for t in range(nt):
            for j in range(len(peers)):
                for half in range(CORES):
                    end_copy(t, half, j).start()

    def cot_copy(x):
        low = x & -x
        held = z if x == low else flipped(z, x - low, chips)
        return pltpu.make_async_remote_copy(
            src_ref=c_v.at[held], dst_ref=c_v.at[held], send_sem=c_ssem.at[x], recv_sem=c_rsem.at[x],
            device_id={"shard": flipped(z, low, chips) * CORES + c}, device_id_type=MESH)

    def p_copy(x, t):
        return pltpu.make_async_remote_copy(
            src_ref=p_send.at[x, t], dst_ref=p_recv.at[x, t], send_sem=p_ssem.at[x, t], recv_sem=p_rsem.at[x, t],
            device_id={"shard": flipped(z, x & -x, chips) * CORES + c}, device_id_type=MESH)

    def s_copy(k):
        return pltpu.make_async_remote_copy(
            src_ref=s_send.at[k], dst_ref=s_recv.at[k],
            send_sem=s_ssem.at[k], recv_sem=s_rsem.at[k],
            device_id={"replica": ahead}, device_id_type=MESH)

    def store(k, i):
        here = pl.ds(pl.multiple_of(k * width, width), width)
        made, out = ((m_v, vel_out), (b_v, mix_out))[i]
        return pltpu.make_async_copy(made.at[here, :], out.at[here, :], store_sem.at[k, i])

    for k in range(nk):
        for half in range(CORES):
            own_copy(k, half).start()

    mine = cur.at[c]
    barrier = pltpu.get_barrier_semaphore()
    for peer in peers:
        pl.semaphore_signal(barrier, inc=1, device_id={"shard": peer * CORES + c}, device_id_type=MESH)
    pl.semaphore_signal(barrier, inc=1, device_id={"replica": behind}, device_id_type=MESH)
    loads[0].wait()
    mine[...] = (b_v[...] / weight[0]).astype(BF16)
    acc[...] = jnp.zeros(acc.shape, F32)
    pl.semaphore_wait(barrier, len(peers) + 1)

    loads[2].wait()
    cot_copy(chips // 2).start()
    loads[3].wait()
    for k in range(min(1, last)):
        send_chunk(k)

    w_send[...] = jnp.full(w_send.shape, weight[0], F32)
    w_copy = pltpu.make_async_remote_copy(
        src_ref=w_send, dst_ref=w_recv, send_sem=w_ssem, recv_sem=w_rsem,
        device_id={"replica": ahead}, device_id_type=MESH)
    w_copy.start()

    bit, sent = chips // 4, min(1, last)
    while bit >= 1:
        for x in range(2 * bit, chips, 4 * bit):
            cot_copy(x).wait_recv()
        for x in range(bit, chips, 2 * bit):
            cot_copy(x).start()
        if sent < min(look, last):
            send_chunk(sent)
            sent += 1
        bit //= 2
    for k in range(sent, min(look, last)):
        send_chunk(k)
    if look >= last:
        send_last()
    loads[1].wait()
    for x in range(1, chips, 2):
        cot_copy(x).wait_recv()
    w_copy.wait()
    w_send[...] = 0.5 * (w_send[...] + w_recv[...])
    w_store = pltpu.make_async_copy(w_send, w_out, w_ssem)
    w_store.start()

    contract = (((0,), (0,)), ((), ()))

    def arrived(k):
        for half in range(CORES):
            own_copy(k, half).wait()
        for j in range(len(peers)):
            for half in range(CORES):
                tok_copy(k, half, j).wait_recv()

    def partial_gradient(k, half):
        t = t_v[k, half].reshape(chips * own_tok, width)
        cots = c_v[...].reshape(chips * own_tok, kv)
        return lax.dot_general(t, cots, contract, preferred_element_type=F32)

    def product(k, t):
        here = pl.ds(pl.multiple_of(k * width, width), width)
        return jnp.dot(t, cur[0, here, :], preferred_element_type=F32)

    def accumulate(k):
        made = product(k, t_v[k, 0].reshape(chips * own_tok, width))
        acc[...] += made.reshape(acc.shape)

    def send_sums(bit, t):
        part = pl.ds(t * block, block)
        for x in range(bit, chips, 2 * bit):
            p_send[x, t] = acc[flipped(z, x, chips), part, :].astype(BF16)
            p_copy(x, t).start()

    def add_sums(bit, t):
        part = pl.ds(t * block, block)
        for x in range(bit, chips, 2 * bit):
            p_copy(x, t).wait_recv()
            acc[flipped(z, x - bit, chips), part, :] += p_recv[x, t].astype(F32)

    bits = [1 << i for i in range(chips.bit_length() - 1)]

    def reduce_step(i, t):
        part = pl.ds(t * block, block)
        if i == 0:
            made = product(last, t_v[last, 0, :, part, :].reshape(chips * block, width))
            acc[:, part, :] += made.reshape(chips, block, kv)
        else:
            add_sums(bits[i - 1], t)
        if i < len(bits):
            send_sums(bits[i], t)
        else:
            p_send[0, t] = acc[z, part, :].astype(BF16)

    def finish_gradient(k):
        here = pl.ds(pl.multiple_of(k * width, width), width)
        gradient = partial_gradient(k, 0) / rep_tok
        velocity = MOMENT * m_v[here, :] + gradient
        m_v[here, :] = velocity
        stepped = b_v[here, :] - LEARN * (gradient + MOMENT * velocity)
        b_v[here, :] = stepped
        s_send[k] = stepped.astype(BF16)
        s_copy(k).start()
        store(k, 0).start()

    def mix(k):
        here = pl.ds(pl.multiple_of(k * width, width), width)
        s_copy(k).wait_recv()
        b_v[here, :] = 0.5 * (b_v[here, :] + s_recv[k].astype(F32))
        store(k, 1).start()

    if nk > 1:
        @pl.loop(0, last)
        def _(k):
            arrived(k)
            finish_gradient(k)

            @pl.when(k + look < last)
            def _():
                send_chunk(k + look)

            @pl.when(k + look == last)
            def _():
                send_last()

            accumulate(k)

            @pl.when(k >= 4)
            def _():
                mix(k - 4)

    for half in range(CORES):
        own_copy(last, half).wait()
    for t in range(nt):
        for j in range(len(peers)):
            for half in range(CORES):
                end_copy(t, half, j).wait_recv()
        reduce_step(0, t)
        if t == nt - 1:
            finish_gradient(last)
        for i in range(1, len(bits) + 1):
            if t >= i:
                reduce_step(i, t - i)
    for k in range(max(0, last - 4), last):
        mix(k)
    for late in range(nt, nt + len(bits)):
        for i in range(1, len(bits) + 1):
            if 0 <= late - i < nt:
                reduce_step(i, late - i)
    p_stores = [
        pltpu.make_async_copy(p_send.at[0, t], p_out.at[pl.ds(t * block, block), :], p_ssem.at[0, t])
        for t in range(nt)
    ]
    for p_store in p_stores:
        p_store.start()
    mix(last)

    for x in range(1, chips):
        cot_copy(x).wait_send()
        for t in range(nt):
            p_copy(x, t).wait_send()
    for j in range(len(peers)):
        for half in range(CORES):
            for k in range(last):
                tok_copy(k, half, j).wait_send()
            for t in range(nt):
                end_copy(t, half, j).wait_send()
    for k in range(nk):
        s_copy(k).wait_send()
        for i in range(2):
            store(k, i).wait()
    w_store.wait()
    for p_store in p_stores:
        p_store.wait()


def push_call(level, chips, tokens, cotangent, numer, moment, weight):
    own_tok, features = tokens.shape
    rows, kv = numer.shape
    nk = max(1, rows // 128)
    nt = max(1, own_tok // 32)
    block = own_tok // nt
    width = rows // nk
    n = chips - 1
    any_spec = pl.BlockSpec(memory_space=pl.ANY)
    dma = pltpu.SemaphoreType.DMA
    return pl.pallas_call(
        partial(push_kernel, 1 << level, chips, nk, 3),
        out_shape=(
            jax.ShapeDtypeStruct((own_tok, kv), BF16),
            jax.ShapeDtypeStruct((rows, kv), F32),
            jax.ShapeDtypeStruct((8, 128), F32),
            jax.ShapeDtypeStruct((rows, kv), F32),
        ),
        in_specs=[any_spec] * 4 + [pl.BlockSpec(memory_space=pltpu.SMEM)],
        out_specs=[any_spec] * 4,
        scratch_shapes=[
            pltpu.VMEM((own_tok, features), BF16),
            pltpu.VMEM((nk, CORES, chips, own_tok, width), BF16),
            pltpu.VMEM((chips, own_tok, kv), BF16),
            pltpu.VMEM((rows, kv), F32),
            pltpu.VMEM((rows, kv), F32),
            pltpu.VMEM((CORES, rows, kv), BF16),
            pltpu.VMEM((chips, own_tok, kv), F32),
            pltpu.VMEM((chips, nt, block, kv), BF16),
            pltpu.VMEM((chips, nt, block, kv), BF16),
            pltpu.VMEM((nk, width, kv), BF16),
            pltpu.VMEM((nk, width, kv), BF16),
            pltpu.VMEM((8, 128), F32),
            pltpu.VMEM((8, 128), F32),
            dma((4,)), dma((nk, CORES)), dma((chips,)), dma((chips,)), dma((nk, CORES, n)), dma((nk, CORES, n)),
            dma((nt, CORES, n)), dma((nt, CORES, n)),
            dma((nk,)), dma((nk,)), dma((chips, nt)), dma((chips, nt)),
            dma(()), dma(()), dma((nk, 2)),
        ],
        compiler_params=pltpu.CompilerParams(
            collective_id=level, has_side_effects=True, vmem_limit_bytes=32 * 1024 * 1024),
        cost_estimate=pl.CostEstimate(
            flops=4 * own_tok * features * kv, bytes_accessed=12 * rows * kv, transcendentals=0),
        name=f"push_round_{level}",
    )(tokens, cotangent, numer, moment, weight)


def hand_out_kernel(parts, p, mix, w, vel, p_out, mix_out, w_out, vel_out, deb_out,
                    p_v, mix_v, w_v, vel_v, deb_v, in_sem, out_sem, small_sem):
    size = mix_v.shape[0] // parts

    def load(i, which):
        here = pl.ds(i * size, size)
        made, held = ((mix, mix_v), (vel, vel_v))[which]
        return pltpu.make_async_copy(made.at[here, :], held.at[here, :], in_sem.at[i, which])

    def store(i, which):
        here = pl.ds(i * size, size)
        held, out = ((mix_v, mix_out), (vel_v, vel_out), (deb_v, deb_out))[which]
        return pltpu.make_async_copy(held.at[here, :], out.at[here, :], out_sem.at[i, which])

    w_load = pltpu.make_async_copy(w, w_v, small_sem.at[0])
    p_load = pltpu.make_async_copy(p, p_v, small_sem.at[1])
    p_store = pltpu.make_async_copy(p_v, p_out, small_sem.at[2])
    w_load.start()
    for i in range(parts):
        load(i, 0).start()
        load(i, 1).start()
    p_load.start()
    w_load.wait()
    scale = w_v[0:1, 0:1]
    w_out[0] = jnp.max(w_v[...])
    for i in range(parts):
        here = pl.ds(i * size, size)
        load(i, 0).wait()
        store(i, 0).start()
        deb_v[here, :] = mix_v[here, :] / scale
        store(i, 2).start()
        load(i, 1).wait()
        store(i, 1).start()
    p_load.wait()
    p_store.start()
    for i in range(parts):
        for which in range(3):
            store(i, which).wait()
    p_store.wait()


def hand_out(p, mix, w, vel):
    any_spec = pl.BlockSpec(memory_space=pl.ANY)
    hbm = pl.BlockSpec(memory_space=pltpu.HBM)
    like = lambda a: jax.ShapeDtypeStruct(a.shape, a.dtype)
    held = lambda a: pltpu.VMEM(a.shape, a.dtype)
    parts = max(1, mix.shape[0] // 128)
    dma = pltpu.SemaphoreType.DMA
    return pl.pallas_call(
        partial(hand_out_kernel, parts),
        out_shape=(like(p), like(mix), jax.ShapeDtypeStruct((1,), F32), like(vel), like(mix)),
        in_specs=[any_spec] * 4,
        out_specs=[hbm, hbm, pl.BlockSpec(memory_space=pltpu.SMEM), hbm, hbm],
        scratch_shapes=[held(p), held(mix), held(w), held(vel), held(mix),
                        dma((parts, 2)), dma((parts, 3)), dma((3,))],
        compiler_params=pltpu.CompilerParams(vmem_limit_bytes=8 * 1024 * 1024),
        cost_estimate=pl.CostEstimate(flops=0, bytes_accessed=12 * mix.size, transcendentals=0),
        name="hand_out",
    )(p, mix, w, vel)


def shards(tokens, cotangent, biased, momentum, weight, round_index):
    hops = lax.axis_size("replica").bit_length() - 1
    chips = lax.axis_size("shard") // CORES
    power = round_index[0] % hops
    branches = [partial(push_call, level, chips) for level in range(hops)]
    made = lax.switch(power, branches, tokens, cotangent, biased[0], momentum[0], weight)
    output, mixed, weight_out, velocity, debiased = hand_out(*made)
    return (output, mixed[None], weight_out, velocity[None], debiased[None])


def solution(mesh):
    placed = (
        P(("replica", "shard"), None),
        P(("replica", "shard"), None),
        P("replica", "shard", None),
        P("replica", "shard", None),
        P("replica"),
        P(),
    )
    return jax.shard_map(
        shards,
        mesh=mesh,
        in_specs=placed,
        out_specs=(
            P(("replica", "shard"), None),
            P("replica", "shard", None),
            P("replica"),
            P("replica", "shard", None),
            P("replica", "shard", None),
        ),
        check_vma=False,
    )
```
